512 devices in a mesh: dp: 16 (over y, x_hi, core), mp: 32 (over z, x_lo).
Axes of the slice: x: 4 (x_hi: 2, x_lo: 2; x = x_hi * 2 + x_lo), y: 4, z: 16, core: 2. Of those that a mesh axis runs over, the one named last changes fastest.
Arguments:
- hidden: bfloat16 [2048, 2048], P('dp')
- head_weight: bfloat16 [126976, 2048], P('mp', 'dp')
- targets: int32 [2048], P('dp'), may hold values from 0 to 126975
- segments: int32 [2048], P('dp'), may hold values from 0 to 63, never falling along the last dimension, each value on 1 to 64 neighbouring positions
- loss_mask: int32 [2048], P('dp'), may hold values 0 or 1
- row_state: float32 [126976], P('mp'), may hold values from 1e-20 to 1e-06
- column_state: float32 [2048], P('dp'), may hold values from 1e-12 to 1e-08
Outputs:
- update_step: bfloat16 [126976, 2048], P('mp', 'dp')
- total_loss: float32 [], replicated
The draws below stay inside these ranges and needn't reach their ends.
Inputs may be any that keep to these rules, and one draw needn't show every extreme that they name: `segments`: segment ids never fall along the tokens; a segment covers 1 to 64 tokens.
All inputs are finite; a program needn't handle non-finite values. No bound on the sum of `loss_mask` on one device may be relied on, other than what follows from the above.
Results may differ from the reference program's by a relative error of at most 0.0039.
Values may be sent and summed in bfloat16 or wider, within the bound.
No kernel may reach another device: no remote copies, remote signals or barrier semaphores. Data moves between devices by JAX's collectives and lax.ppermute only.
A program may use at most 128 MiB of HBM per device.

```python
import math
import jax
import jax.numpy as jnp
import numpy as np
from jax import lax

D = 2048
V = 126976
SEG_MOST = 64
TOKENS = 2048
SEGS = 64
N_MP = 32


aligned_score = 150.0


def base_head(key):
    return jax.random.normal(key, (V, D), jnp.float32) * (3.0 / math.sqrt(D))


def drawn_picks(key):
    picked = jax.random.fold_in(key, 11)
    first_key, second_key, third_key, fourth_key = jax.random.split(picked, 4)
    positions = jax.random.randint(first_key, (8,), 0, TOKENS)
    vocab_rows = jax.random.randint(second_key, (8,), 0, V // 2) * 2
    strengths = (0.8 + 0.17 * jnp.arange(8, dtype=jnp.float32)) * jax.random.uniform(third_key, (8,), jnp.float32, 0.97, 1.03)
    margins = jax.random.uniform(fourth_key, (8,), jnp.float32, 1.5, 2.5)
    return (positions, vocab_rows, strengths, margins)


def draw_head_weight(key, part):
    weights = base_head(key)
    positions, vocab_rows, strengths, margins = drawn_picks(key)
    shrink = 1.0 - margins / (strengths * aligned_score)
    weights = weights.at[vocab_rows + 1].set(weights[vocab_rows] * shrink[:, None])
    return weights.astype(jnp.bfloat16)


def draw_hidden(key, part):
    base_key = key
    key = jax.random.fold_in(key, 3)
    values = jax.random.normal(key, (TOKENS, D), jnp.float32) * 0.5
    common = jax.random.normal(jax.random.fold_in(key, 5), (1, D), jnp.float32) * 0.9
    values = values + common
    weights = base_head(base_key)
    positions, vocab_rows, strengths, margins = drawn_picks(base_key)
    values = values.at[positions].set(strengths[:, None] * weights[vocab_rows] * (aligned_score / 9.0))
    return values.astype(jnp.bfloat16)


def with_ends(values, rng, low, largest):
    spot = [jax.random.randint(jax.random.fold_in(rng, axis), (), 0, length) for axis, length in enumerate(values.shape)]
    longest = values.shape.index(max(values.shape))
    next_to = spot[:longest] + [(spot[longest] + 1) % values.shape[longest]] + spot[longest + 1:]
    return values.at[tuple(spot)].set(low).at[tuple(next_to)].set(largest)


def shard_levels(key, extent, cuts, smallest, high):
    loudness, own = 1.0, jax.random.fold_in(key, 6)
    for position, parts in cuts:
        heights = jnp.exp(jax.random.uniform(jax.random.fold_in(own, position), (parts,), jnp.float32, smallest / len(cuts), high / len(cuts)))
        loudness = loudness * jnp.repeat(heights, extent[position] // parts).reshape([-1 if axis == position else 1 for axis in range(len(extent))])
    return loudness


def ranked_wide(rng, extent, number_of, skew):
    portions = [min(1 << octave, number_of + 1 - (1 << octave)) * (1 << 20) // math.isqrt((1 << octave) ** skew) + 1 for octave in range((number_of + 1).bit_length()) if 1 << octave <= number_of]
    deviation = 1 + sum(portions) // (1 << 30)
    table = np.cumsum(np.array([max(1, weight // deviation) for weight in portions]))
    ticket = jax.random.randint(jax.random.fold_in(rng, 1), extent, 0, int(table[len(portions) - 1]))
    start = jnp.left_shift(1, jnp.searchsorted(jnp.asarray(table, jnp.int32), ticket, side="right").astype(jnp.int32))
    standing = start - 1 + jax.random.randint(jax.random.fold_in(rng, 4), extent, 0, 1 << 30) % jnp.minimum(start, number_of + 1 - start)
    return jax.random.permutation(jax.random.fold_in(rng, 2), number_of)[standing].astype(jnp.int32)


def length_profile(amount, total, reach, slope):
    loads = [(1 << 20) // math.isqrt(grade ** slope) + 1 for grade in range(2, amount + 1)]
    surplus, given = total - reach - (amount - 1), [1] * (amount - 1)
    while surplus > 0:
        candidates = [i for i in range(amount - 1) if given[i] < reach]
        pool, budget = sum([loads[i] for i in candidates]), surplus
        for i in candidates:
            addition = min(reach - given[i], max(1, budget * loads[i] // pool), surplus)
            given[i] = given[i] + addition
            surplus = surplus - addition
    return np.array([reach] + given)


def ragged(rng, amount, total, most, skew):
    if amount == 2:
        one = jax.random.randint(rng, (), max(1, total - most), min(most, total - 1) + 1)
        return jnp.stack([one, total - one])
    sizes = jnp.asarray(length_profile(amount, total, most, skew), jnp.int32)
    twos = (amount - 1) // 2
    source_of, sink = sizes[1:1 + 2 * twos:2], sizes[2:2 + 2 * twos:2]
    slack = jnp.minimum(source_of - 1, most - sink)
    moved = jax.random.randint(jax.random.fold_in(rng, 1), (twos,), 0, 1 << 20) % (slack + 1)
    sizes = sizes.at[1:1 + 2 * twos:2].set(source_of - moved).at[2:2 + 2 * twos:2].set(sink + moved)
    return sizes[jax.random.permutation(jax.random.fold_in(rng, 2), amount)]


def setup_inputs(seed: int = 0) -> dict:
    seeds = jax.random.split(jax.random.key(seed), 8)
    hidden = draw_hidden(jax.random.fold_in(seeds[7], 71), 0)
    head_weight = draw_head_weight(jax.random.fold_in(seeds[7], 71), 0)
    targets = with_ends(ranked_wide(seeds[2], (TOKENS,), V, 2), jax.random.fold_in(seeds[2], 3), 0, V - 1).astype(jnp.int32)
    segments = jnp.searchsorted(jnp.cumsum(ragged(seeds[3], SEGS, TOKENS, SEG_MOST, 2)), jnp.arange(TOKENS), side="right").astype(jnp.int32)
    loss_mask = with_ends((jax.random.randint(seeds[4], (TOKENS,), 0, 4) < 3).astype(jnp.int32), jax.random.fold_in(seeds[4], 1), 0, 1)
    row_state = jnp.clip(jnp.exp(math.log(9.999999974752427e-07) - 32.23619 * jax.random.uniform(seeds[5], (V,), jnp.float32) ** shard_levels(seeds[5], (V,), ((0, 32),), -0.2, 0.2)), 9.999999682655225e-21, 9.999999974752427e-07)
    column_state = jnp.clip(jnp.exp(math.log(9.99999993922529e-09) - 9.2103404 * jax.random.uniform(seeds[6], (D,), jnp.float32) ** shard_levels(seeds[6], (D,), ((0, 16),), -0.2, 0.2)), 9.999999960041972e-13, 9.99999993922529e-09)
    return dict(hidden=hidden, head_weight=head_weight, targets=targets, segments=segments, loss_mask=loss_mask, row_state=row_state, column_state=column_state)


penalty = 0.25
decay_rate = 1.0 - 16.0 ** (-0.8)
clip_limit = 1.0

def reference(hidden, head_weight, targets, segments, loss_mask, row_state, column_state):
    block_size = V // N_MP
    seg_count = TOKENS // 32
    mask_value = loss_mask.astype(jnp.float32)
    member = (segments[:, None] == jnp.arange(seg_count, dtype=jnp.int32)[None, :]).astype(jnp.float32)
    counts = lax.optimization_barrier(jnp.sum(member * mask_value[:, None], axis=0))
    tok_weight = mask_value / jnp.maximum(lax.optimization_barrier(jnp.sum(member * counts[None, :], axis=1)), 1.0) / seg_count
    head_blocks = head_weight.reshape(N_MP, block_size, D)
    offsets = jnp.arange(N_MP, dtype=jnp.int32) * block_size

    def block_scores(block_rows):
        return jnp.dot(hidden, block_rows.T, preferred_element_type=jnp.float32)

    def first_pass(running, packed):
        block_rows, offset = packed
        row_max, exp_sum, exp_dot, target_logit = running
        logits = block_scores(block_rows)
        new_max = jnp.maximum(row_max, lax.optimization_barrier(jnp.max(logits, axis=1)))
        factor = jnp.exp(row_max - new_max)
        shifted = jnp.exp(logits - new_max[:, None])
        target_hit = jnp.arange(block_size, dtype=jnp.int32)[None, :] + offset == targets[:, None]
        exp_sum = exp_sum * factor + lax.optimization_barrier(jnp.sum(shifted, axis=1))
        exp_dot = exp_dot * factor + lax.optimization_barrier(jnp.sum(shifted * logits, axis=1))
        target_logit = target_logit + lax.optimization_barrier(jnp.sum(jnp.where(target_hit, logits, jnp.float32(0.0)), axis=1))
        return ((new_max, exp_sum, exp_dot, target_logit), None)
    starting = (jnp.full((TOKENS,), -1e+30, jnp.float32), jnp.zeros((TOKENS,), jnp.float32), jnp.zeros((TOKENS,), jnp.float32), jnp.zeros((TOKENS,), jnp.float32))
    totals, unused = lax.scan(first_pass, starting, (head_blocks, offsets))
    row_max, exp_sum, exp_dot, target_logit = totals
    log_total = row_max + jnp.log(exp_sum)
    entropy = log_total - exp_dot / exp_sum
    token_loss = log_total - target_logit - penalty * entropy
    total_loss = jnp.sum(tok_weight * token_loss)

    def second_pass(running, packed):
        block_rows, offset = packed
        logits = block_scores(block_rows)
        probability = jnp.exp(logits - log_total[:, None])
        target_hit = (jnp.arange(block_size, dtype=jnp.int32)[None, :] + offset == targets[:, None]).astype(jnp.float32)
        score_grad = (tok_weight[:, None] * (probability - target_hit + penalty * probability * (logits - log_total[:, None] + entropy[:, None]))).astype(jnp.bfloat16)
        block_grad = jnp.dot(score_grad.T, hidden, preferred_element_type=jnp.float32)
        return (running, block_grad)
    unused_two, grad_blocks = lax.scan(second_pass, jnp.float32(0.0), (head_blocks, offsets))
    head_grad = grad_blocks.reshape(V, D)
    squared = head_grad * head_grad
    row_new = decay_rate * row_state + (1.0 - decay_rate) * (lax.optimization_barrier(jnp.sum(squared, axis=1)) / D)
    column_new = decay_rate * column_state + (1.0 - decay_rate) * (lax.optimization_barrier(jnp.sum(squared, axis=0)) / V)
    row_mean = jnp.sum(row_new) / V
    unclipped = head_grad * lax.rsqrt(row_new)[:, None] * (jnp.sqrt(row_mean) * lax.rsqrt(column_new))[None, :]
    update_rms = jnp.sqrt(jnp.sum(unclipped * unclipped) / (V * D))
    update_step = (unclipped / jnp.maximum(1.0, update_rms / clip_limit)).astype(jnp.bfloat16)
    return (update_step, total_loss)
```

```python
import jax
import jax.numpy as jnp
from jax import lax
from jax.sharding import Mesh, PartitionSpec as P

D = 2048
V = 126976

penalty = 0.25
decay_rate = 1.0 - 16.0 ** (-0.8)
clip_limit = 1.0

AXES = ("y", "xh", "core", "z", "xl")
DP = ("y", "xh", "core")
MP = ("z", "xl")
CHIPS = ("y", "xh")
PLANE = ("y", "xh", "xl")


def swap_cores(value):
    return lax.ppermute(value, "core", [(0, 1), (1, 0)])


def spread(value, axes):
    count = lax.axis_size(axes)
    return lax.all_to_all(
        jnp.broadcast_to(value[None], (count,) + value.shape), axes, 0, 0
    )


def pieces(value):
    high = lax.reduce_precision(value, 8, 7)
    rest = value - high
    middle = lax.reduce_precision(rest, 8, 7)
    low = rest - middle
    return [part.astype(jnp.bfloat16) for part in (high, middle, low)]


def merge_scores(stats):
    row_max = jnp.max(stats[:, 0], axis=0)
    factor = jnp.exp(stats[:, 0] - row_max[None])
    return jnp.stack(
        [
            row_max,
            jnp.sum(stats[:, 1] * factor, axis=0),
            jnp.sum(stats[:, 2] * factor, axis=0),
            jnp.sum(stats[:, 3], axis=0),
        ]
    )


def per_device(hidden, head_weight, targets, segments, loss_mask, row_state, column_state):
    tok_rows = hidden.shape[0]
    voc_rows, cols = head_weight.shape
    chips = lax.axis_size(CHIPS)
    seg_count = tok_rows * chips * 2 // 32
    chip_rows = voc_rows // chips
    own_rows = chip_rows // 2
    core = lax.axis_index("core")
    chip = lax.axis_index(CHIPS)
    row_start = lax.axis_index(MP) * voc_rows + chip * chip_rows

    info = jnp.stack(
        [
            (targets >> 16).astype(jnp.bfloat16),
            ((targets >> 8) & 255).astype(jnp.bfloat16),
            (targets & 255).astype(jnp.bfloat16),
            segments.astype(jnp.bfloat16),
            loss_mask.astype(jnp.bfloat16),
        ]
        + pieces(column_state)
    )
    info = jnp.concatenate([info, jnp.zeros_like(info)], axis=0)
    head_part = jnp.concatenate(
        [
            head_weight.reshape(chips, chip_rows, cols),
            jnp.broadcast_to(info[None], (chips,) + info.shape),
        ],
        axis=1,
    )
    tall = chip_rows + 16
    wide = D // cols
    head_part = (
        head_part.reshape(chips, tall // wide // 16, wide, 16, cols)
        .transpose(0, 1, 3, 2, 4)
        .reshape(chips, tall // wide, D)
    )
    sent = jnp.concatenate(
        [jnp.broadcast_to(hidden[None], (chips,) + hidden.shape), head_part], axis=1
    )
    got = lax.all_to_all(sent, CHIPS, 0, 0)
    hidden_own = got[:, :tok_rows].reshape(chips * tok_rows, D)
    head_got = (
        got[:, tok_rows:]
        .reshape(chips, tall // wide // 16, 16, wide, cols)
        .transpose(0, 1, 3, 2, 4)
        .reshape(chips, tall, cols)
    )
    head_other = swap_cores(head_got)
    both = jnp.where(
        core == 0,
        jnp.stack([head_got, head_other], axis=1),
        jnp.stack([head_other, head_got], axis=1),
    )
    rows = both[:, :, :chip_rows].transpose(2, 0, 1, 3).reshape(chip_rows, D)
    facts = both[:, :, chip_rows : chip_rows + 8].astype(jnp.float32)

    all_segments = facts[:, :, 3]
    all_masks = facts[:, :, 4]
    own_facts = lax.dynamic_index_in_dim(facts, core, axis=1, keepdims=False)
    own_segments = own_facts[:, 3].reshape(-1)
    own_mask = own_facts[:, 4].reshape(-1)
    own_targets = (
        own_facts[:, 0] * 65536.0 + own_facts[:, 1] * 256.0 + own_facts[:, 2]
    ).reshape(-1).astype(jnp.int32)
    seg_ids = jnp.arange(seg_count, dtype=jnp.int32).astype(jnp.float32)
    counts = jnp.sum(
        jnp.where(
            all_segments.reshape(1, -1) == seg_ids[:, None], all_masks.reshape(1, -1), 0.0
        ),
        axis=1,
    )
    own_counts = jnp.sum(
        jnp.where(own_segments[None, :] == seg_ids[:, None], counts[:, None], 0.0), axis=0
    )
    tok_weight = own_mask / jnp.maximum(own_counts, 1.0) / seg_count
    full_column_state = (facts[:, :, 5] + facts[:, :, 6] + facts[:, :, 7]).reshape(-1)

    logits = lax.dot_general(
        rows, hidden_own, (((1,), (1,)), ((), ())), preferred_element_type=jnp.float32
    )
    target_hit = (
        jnp.arange(chip_rows, dtype=jnp.int32)[:, None] + row_start == own_targets[None, :]
    )
    local_max = jnp.max(logits, axis=0)
    shifted = jnp.exp(logits - local_max[None])
    stats = jnp.stack(
        [
            local_max,
            jnp.sum(shifted, axis=0),
            jnp.sum(shifted * logits, axis=0),
            jnp.sum(jnp.where(target_hit, logits, 0.0), axis=0),
        ]
    )
    hidden_other = swap_cores(hidden_own)
    stats = merge_scores(spread(stats, PLANE))
    row_max, exp_sum, exp_dot, target_logit = merge_scores(spread(stats, "z"))
    log_total = row_max + jnp.log(exp_sum)
    entropy = log_total - exp_dot / exp_sum
    token_loss = log_total - target_logit - penalty * entropy
    local_loss = jnp.sum(tok_weight * token_loss)

    probability = jnp.exp(logits - log_total[None])
    score_grad = (
        tok_weight[None]
        * (
            probability
            - target_hit.astype(jnp.float32)
            + penalty * probability * (logits - log_total[None] + entropy[None])
        )
    ).astype(jnp.bfloat16)
    score_halves = score_grad.reshape(2, own_rows, -1)
    score_own = lax.dynamic_index_in_dim(score_halves, core, axis=0, keepdims=False)
    score_away = lax.dynamic_index_in_dim(score_halves, 1 - core, axis=0, keepdims=False)
    score_other = swap_cores(score_away)
    head_grad = lax.dot_general(
        score_own, hidden_own, (((1,), (0,)), ((), ())), preferred_element_type=jnp.float32
    ) + lax.dot_general(
        score_other, hidden_other, (((1,), (0,)), ((), ())), preferred_element_type=jnp.float32
    )
    squared = head_grad * head_grad
    own_state = lax.dynamic_slice_in_dim(
        row_state, chip * chip_rows + core * own_rows, own_rows, axis=0
    )
    row_new = decay_rate * own_state + (1.0 - decay_rate) * (jnp.sum(squared, axis=1) / D)
    scaled = head_grad * lax.rsqrt(row_new)[:, None]
    tail = jnp.zeros((cols,), jnp.float32).at[0].set(jnp.sum(row_new)).at[1].set(local_loss)
    sums = jnp.concatenate([jnp.sum(squared, axis=0), jnp.sum(scaled * scaled, axis=0), tail])
    sums = lax.psum(sums.reshape(-1, cols), "core")
    total_loss = sums[-1, 1]
    sums = jnp.sum(spread(sums, PLANE), axis=0)
    sums = jnp.sum(spread(sums, "z"), axis=0).reshape(-1)
    column_new = decay_rate * full_column_state + (1.0 - decay_rate) * (sums[:D] / V)
    row_mean = sums[2 * D] / V
    column_scale = lax.rsqrt(column_new)
    square_total = row_mean * jnp.sum(sums[D : 2 * D] * column_scale * column_scale)
    update_rms = jnp.sqrt(square_total / (V * D))
    factor = jnp.sqrt(row_mean) * column_scale / jnp.maximum(1.0, update_rms / clip_limit)
    update = (scaled * factor[None]).astype(jnp.bfloat16)
    update = update.reshape(own_rows, 2 * chips, cols).transpose(1, 0, 2)
    update_step = lax.all_to_all(update, DP, 0, 0).reshape(voc_rows, cols)
    return (update_step, total_loss)


def solution(mesh):
    fine = Mesh(mesh.devices.reshape(4, 2, 2, 16, 2), AXES)
    return jax.shard_map(
        per_device,
        mesh=fine,
        in_specs=(P(DP, None), P(MP, DP), P(DP), P(DP), P(DP), P(MP), P(DP)),
        out_specs=(P(MP, DP), P()),
        check_vma=False,
    )
```

```python
import jax
import jax.numpy as jnp
from jax import lax
from jax.experimental import pallas as pl
from jax.experimental.pallas import tpu as pltpu
from jax.sharding import Mesh, PartitionSpec as P

D = 2048
V = 126976

penalty = 0.25
decay_rate = 1.0 - 16.0 ** (-0.8)
clip_limit = 1.0

AXES = ("y", "xh", "core", "z", "xl")
DP = ("y", "xh", "core")
MP = ("z", "xl")
CHIPS = ("y", "xh")
PLANE = ("y", "xh", "xl")

PEERS = 8
TOK = 128
COLS = 128
VOC = 3968
CHIP_ROWS = 496
OWN = 248
PAD = 256
TOKENS = 1024
SEGS = 64
STEP = 6 * 128
LAST = 4 * 128
f32 = jnp.float32
bf16 = jnp.bfloat16

params = pltpu.CompilerParams(vmem_limit_bytes=24 * 1024 * 1024)
VMEM = pl.BlockSpec(memory_space=pltpu.VMEM)
SMEM = pl.BlockSpec(memory_space=pltpu.SMEM)


def swap_cores(value):
    return lax.ppermute(value, "core", [(0, 1), (1, 0)])


def trade(value, axes):
    return lax.all_to_all(value, axes, 0, 0)


def pack_kernel(hidden, head, targets, segments, mask, state, out):
    out[0, :TOK, :] = hidden[...]
    for block in range(4):
        height = min(128, CHIP_ROWS - 128 * block)
        out[0, TOK : TOK + height, 128 * block : 128 * block + 128] = head[
            128 * block : 128 * block + height, :
        ]
    row = lax.broadcasted_iota(jnp.int32, (16, 128), 0)
    goal = targets[...]
    value = state[...]
    high = value.astype(bf16).astype(f32)
    rest = value - high
    middle = rest.astype(bf16).astype(f32)
    facts = jnp.zeros((16, 128), f32)
    for place, fact in enumerate(
        [
            (goal >> 16).astype(f32),
            ((goal >> 8) & 255).astype(f32),
            (goal & 255).astype(f32),
            segments[...].astype(f32),
            mask[...].astype(f32),
            high,
            middle,
            rest - middle,
        ]
    ):
        facts = jnp.where(row == place, fact, facts)
    out[0, 2 * TOK - 16 :, LAST - 128 :] = facts.astype(bf16)


def pack(hidden, head, targets, segments, mask, state):
    small = pl.BlockSpec((1, 128), lambda i: (0, 0))
    return pl.pallas_call(
        pack_kernel,
        grid=(PEERS,),
        in_specs=[
            pl.BlockSpec((TOK, LAST), lambda i: (0, 3)),
            pl.BlockSpec((CHIP_ROWS, COLS), lambda i: (i, 0)),
            small,
            small,
            small,
            small,
        ],
        out_specs=pl.BlockSpec((1, 2 * TOK, LAST), lambda i: (i, 0, 0)),
        out_shape=jax.ShapeDtypeStruct((PEERS, 2 * TOK, LAST), bf16),
        compiler_params=params,
        name="pack",
    )(hidden, head, *[x.reshape(1, 128) for x in (targets, segments, mask, state)])


def gather_weight(source, rows, weight):
    def one(q, carry):
        columns = pl.ds(pl.multiple_of(q * 128, 128), 128)
        for block in range(4):
            height = min(128, CHIP_ROWS - 128 * block)
            weight[128 * block : 128 * block + height, columns] = source[
                q, rows : rows + height, 128 * block : 128 * block + 128
            ]
        return carry

    lax.fori_loop(0, PEERS, one, 0)


def half_kernel(place, first, near, far, last, hidden, partial, weight):
    core = place[0]
    odd = place[2]

    def fill(source, rows, index, start, count):
        for i in range(count):
            column = start + i // 2 + 8 * (core if i % 2 == 0 else 1 - core)
            hidden[rows, pl.ds(pl.multiple_of(column * 128, 128), 128)] = source[
                index, :TOK, 128 * i : 128 * i + 128
            ]

    def one(q, carry):
        rows = pl.ds(pl.multiple_of(q * TOK, TOK), TOK)
        fill(first, rows, q, 3 * odd, 6)
        fill(last, rows, q, 6, 4)
        return carry

    def two(q, carry):
        fill(near, pl.ds(pl.multiple_of(q * TOK, TOK), TOK), q, 3 - 3 * odd, 6)
        fill(far, pl.ds(pl.multiple_of((q + 4) * TOK, TOK), TOK), q, 3 - 3 * odd, 6)
        return carry

    lax.fori_loop(0, PEERS, one, 0)
    lax.fori_loop(0, PEERS // 2, two, 0)
    gather_weight(last, TOK, weight)
    for block in range(4):
        tokens = slice(256 * block, 256 * block + 256)
        partial[:, tokens] = lax.dot_general(
            weight[...],
            hidden[tokens, : D // 2],
            (((1,), (1,)), ((), ())),
            preferred_element_type=f32,
        )


def half_call(place, first, near, far, last):
    return pl.pallas_call(
        half_kernel,
        in_specs=[SMEM, VMEM, VMEM, VMEM, VMEM],
        out_specs=[VMEM, VMEM],
        out_shape=[
            jax.ShapeDtypeStruct((TOKENS, D), bf16),
            jax.ShapeDtypeStruct((CHIP_ROWS, TOKENS), f32),
        ],
        scratch_shapes=[pltpu.VMEM((CHIP_ROWS, D // 2), bf16)],
        compiler_params=params,
        cost_estimate=pl.CostEstimate(
            flops=10**11, bytes_accessed=10**8, transcendentals=0
        ),
        name="half",
    )(place, first, near, far, last)


def logits_kernel(
    place, hidden, partial, own, other, logits, stats, tokens, state, weight, facts, counts
):
    step = pl.program_id(0)
    core = place[0]
    row_start = place[1]

    @pl.when(step == 0)
    def _():
        gather_weight(other, 0, weight)
        for q in range(PEERS):
            facts[2 * q + core] = own[q, 2 * TOK - 16 :, LAST - 128 :].astype(f32)
            facts[2 * q + 1 - core] = other[q, TOK - 16 :, LAST - 128 :].astype(f32)
        seg = lax.broadcasted_iota(jnp.int32, (SEGS, 128), 0).astype(f32)
        total = jnp.zeros((SEGS, 128), f32)
        for j in range(2 * PEERS):
            total = total + jnp.where(facts[j, 3:4, :] == seg, facts[j, 4:5, :], 0.0)
            state[j : j + 1, :] = facts[j, 5:6, :] + facts[j, 6:7, :] + facts[j, 7:8, :]
        counts[...] = jnp.broadcast_to(jnp.sum(total, axis=1, keepdims=True), (SEGS, 128))

    scores = partial[...] + lax.dot_general(
        weight[...], hidden[...], (((1,), (1,)), ((), ())), preferred_element_type=f32
    )
    logits[:CHIP_ROWS, :] = scores
    logits[CHIP_ROWS:, :] = jnp.zeros((8, 2 * TOK), f32)
    seg = lax.broadcasted_iota(jnp.int32, (SEGS, 128), 0).astype(f32)
    row = lax.broadcasted_iota(jnp.int32, (CHIP_ROWS, 128), 0) + row_start
    tokens[...] = jnp.zeros_like(tokens)
    for half in range(2):
        part = scores[:, half * 128 : half * 128 + 128]
        q = step * 2 + half
        fact = facts[2 * q + core]
        top = jnp.max(part, axis=0, keepdims=True)
        shifted = jnp.exp(part - top)
        exp_sum = jnp.sum(shifted, axis=0, keepdims=True)
        exp_dot = jnp.sum(shifted * part, axis=0, keepdims=True)
        goal = fact[0:1] * 65536.0 + fact[1:2] * 256.0 + fact[2:3]
        hit = row == goal.astype(jnp.int32)
        target_logit = jnp.sum(jnp.where(hit, part, 0.0), axis=0, keepdims=True)
        own_count = jnp.sum(
            jnp.where(fact[3:4] == seg, counts[...], 0.0), axis=0, keepdims=True
        )
        tok_weight = fact[4:5] / jnp.maximum(own_count, 1.0) / SEGS
        lanes = slice(half * 128, half * 128 + 128)
        tokens[0:1, lanes] = tok_weight
        tokens[1:2, lanes] = goal
        tokens[2:3, lanes] = tok_weight * target_logit
        partial_total = top + jnp.log(exp_sum)
        mean = exp_dot / exp_sum
        for peer in range(16):
            stats[peer, pl.ds(q, 1), :] = partial_total
            stats[peer, pl.ds(8 + q, 1), :] = mean


def logits_call(place, hidden, partial, own, other):
    return pl.pallas_call(
        logits_kernel,
        grid=(4,),
        in_specs=[
            SMEM,
            pl.BlockSpec((2 * TOK, D // 2), lambda i: (i, 1)),
            pl.BlockSpec((CHIP_ROWS, 2 * TOK), lambda i: (0, i)),
            pl.BlockSpec((PEERS, 2 * TOK, LAST), lambda i: (0, 0, 0)),
            pl.BlockSpec((PEERS, TOK, LAST), lambda i: (0, 0, 0)),
        ],
        out_specs=[
            pl.BlockSpec((CHIP_ROWS + 8, 2 * TOK), lambda i: (0, i)),
            pl.BlockSpec((16, 16, 128), lambda i: (0, 0, 0)),
            pl.BlockSpec((8, 2 * TOK), lambda i: (0, i)),
            pl.BlockSpec((16, 128), lambda i: (0, 0)),
        ],
        out_shape=[
            jax.ShapeDtypeStruct((CHIP_ROWS + 8, TOKENS), f32),
            jax.ShapeDtypeStruct((16, 16, 128), f32),
            jax.ShapeDtypeStruct((8, TOKENS), f32),
            jax.ShapeDtypeStruct((16, 128), f32),
        ],
        scratch_shapes=[
            pltpu.VMEM((CHIP_ROWS, D // 2), bf16),
            pltpu.VMEM((16, 16, 128), f32),
            pltpu.VMEM((SEGS, 128), f32),
        ],
        compiler_params=params,
        name="logits",
    )(place, hidden, partial, own, other)


def merged(stats):
    part, mean = stats[:, :8, :], stats[:, 8:, :]
    top = jnp.max(part, axis=0)
    share = jnp.exp(part - top[None])
    total = jnp.sum(share, axis=0)
    return top + jnp.log(total), jnp.sum(share * mean, axis=0) / total


def merge_kernel(stats, out):
    log_total, mean = merged(stats[...])
    out[:, :8, :] = jnp.broadcast_to(log_total[None], (16, 8, 128))
    out[:, 8:, :] = jnp.broadcast_to(mean[None], (16, 8, 128))


def merge_call(stats):
    return pl.pallas_call(
        merge_kernel,
        in_specs=[VMEM],
        out_specs=VMEM,
        out_shape=jax.ShapeDtypeStruct((16, 16, 128), f32),
        compiler_params=params,
        name="merge",
    )(stats)


def score_block(logits, tokens, log_total, entropy, base, row_start, q):
    lanes = slice(q * 128, q * 128 + 128)
    part = logits[pl.ds(pl.multiple_of(base, 8), PAD), lanes]
    row = lax.broadcasted_iota(jnp.int32, (PAD, 128), 0)
    tok_weight = tokens[0:1, lanes]
    goal = tokens[1:2, lanes].astype(jnp.int32)
    hit = (row + (row_start + base) == goal).astype(f32)
    above = part - log_total[q : q + 1, :]
    probability = jnp.exp(above)
    score = tok_weight * (
        probability - hit + penalty * probability * (above + entropy[q : q + 1, :])
    )
    return jnp.where(row < OWN, score, 0.0).astype(bf16)


def away_kernel(place, stats, logits, tokens, score, totals):
    core = place[0]
    log_total, mean = merged(stats[...])
    entropy = log_total - mean
    totals[:8, :] = log_total
    totals[8:, :] = entropy
    for q in range(PEERS):
        score[:, q * 128 : q * 128 + 128] = score_block(
            logits, tokens, log_total, entropy, (1 - core) * OWN, place[1], q
        )


def away_call(place, stats, logits, tokens):
    return pl.pallas_call(
        away_kernel,
        in_specs=[SMEM, VMEM, VMEM, VMEM],
        out_specs=[VMEM, VMEM],
        out_shape=[
            jax.ShapeDtypeStruct((PAD, TOKENS), bf16),
            jax.ShapeDtypeStruct((16, 128), f32),
        ],
        compiler_params=params,
        name="away",
    )(place, stats, logits, tokens)


def own_kernel(place, totals, logits, tokens, hidden, out, score):
    @pl.when(pl.program_id(0) == 0)
    def _():
        for q in range(PEERS):
            score[:, q * 128 : q * 128 + 128] = score_block(
                logits, tokens, totals[:8, :], totals[8:, :], place[0] * OWN, place[1], q
            )

    out[...] = jnp.dot(score[...], hidden[...], preferred_element_type=f32)


def own_call(place, totals, logits, tokens, hidden):
    return pl.pallas_call(
        own_kernel,
        grid=(4,),
        in_specs=[
            SMEM,
            pl.BlockSpec((16, 128), lambda i: (0, 0)),
            pl.BlockSpec((CHIP_ROWS + 8, TOKENS), lambda i: (0, 0)),
            pl.BlockSpec((8, TOKENS), lambda i: (0, 0)),
            pl.BlockSpec((TOKENS, 512), lambda i: (0, i)),
        ],
        out_specs=pl.BlockSpec((PAD, 512), lambda i: (0, i)),
        out_shape=jax.ShapeDtypeStruct((PAD, D), f32),
        scratch_shapes=[pltpu.VMEM((PAD, TOKENS), bf16)],
        compiler_params=params,
        name="own",
    )(place, totals, logits, tokens, hidden)


def split_rows(value):
    high = value.astype(bf16).astype(f32)
    rest = value - high
    middle = rest.astype(bf16).astype(f32)
    return [high, middle, rest - middle]


def join_rows(total, start):
    return total[start : start + 1] + total[start + 1 : start + 2] + total[start + 2 : start + 3]


def grad_kernel(
    place, partial, score, hidden, state, totals, tokens, scaled, sums, grad, table
):
    step = pl.program_id(0)
    value = partial[...] + jnp.dot(score[...], hidden[...], preferred_element_type=f32)
    grad[:, pl.ds(pl.multiple_of(step * 512, 512), 512)] = value

    @pl.when(step == 3)
    def _():
        core = place[0]
        places = [2 * i + core for i in range(8)] + [2 * i + 1 - core for i in range(8)]
        squares = jnp.zeros((PAD, 128), f32)
        for i, j in enumerate(places):
            part = grad[:, 128 * i : 128 * i + 128]
            part = part * part
            squares = squares + part
            table[pl.ds(j, 1), :] = jnp.sum(part, axis=0, keepdims=True)
        row_new = decay_rate * state[...] + (1.0 - decay_rate) * (
            jnp.sum(squares, axis=1, keepdims=True) / D
        )
        scale = jnp.broadcast_to(lax.rsqrt(row_new), (PAD, 128))
        row = lax.broadcasted_iota(jnp.int32, (PAD, 128), 0)
        lane = lax.broadcasted_iota(jnp.int32, (PAD, 128), 1)
        kept = jnp.where(
            (row < OWN) & (lane == 0), jnp.broadcast_to(row_new, (PAD, 128)), 0.0
        )
        row_total = jnp.sum(kept, axis=0, keepdims=True)
        loss = jnp.zeros((1, 128), f32)
        for q in range(PEERS):
            lanes = slice(128 * q, 128 * q + 128)
            loss = loss + (
                tokens[0:1, lanes]
                * (totals[q : q + 1, :] - penalty * totals[8 + q : 9 + q, :])
                * (1.0 / 256.0)
                - tokens[2:3, lanes]
            )
        table[32:48, :] = jnp.zeros((16, 128), f32)
        for i, line in enumerate(split_rows(row_total) + split_rows(loss)):
            table[32 + i : 33 + i, :] = line
        for i, j in enumerate(places):
            part = grad[:, 128 * i : 128 * i + 128] * scale
            scaled[:, pl.ds(pl.multiple_of(j * 128, 128), 128)] = part
            table[pl.ds(16 + j, 1), :] = jnp.sum(part * part, axis=0, keepdims=True)
        sums[...] = jnp.broadcast_to(table[...].astype(bf16)[None], (32, 48, 128))


def grad_call(place, partial, score, hidden, state, totals, tokens):
    return pl.pallas_call(
        grad_kernel,
        grid=(4,),
        in_specs=[
            SMEM,
            pl.BlockSpec((PAD, 512), lambda i: (0, i)),
            pl.BlockSpec((PAD, TOKENS), lambda i: (0, 0)),
            pl.BlockSpec((TOKENS, 512), lambda i: (0, (i + 2) % 4)),
            pl.BlockSpec((PAD, 1), lambda i: (0, 0)),
            pl.BlockSpec((16, 128), lambda i: (0, 0)),
            pl.BlockSpec((8, TOKENS), lambda i: (0, 0)),
        ],
        out_specs=[
            pl.BlockSpec((PAD, D), lambda i: (0, 0)),
            pl.BlockSpec((32, 48, 128), lambda i: (0, 0, 0)),
        ],
        out_shape=[
            jax.ShapeDtypeStruct((PAD, D), f32),
            jax.ShapeDtypeStruct((32, 48, 128), bf16),
        ],
        scratch_shapes=[pltpu.VMEM((PAD, D), f32), pltpu.VMEM((48, 128), f32)],
        compiler_params=params,
        name="grad",
    )(place, partial, score, hidden, state, totals, tokens)


def add_kernel(sums, out):
    total = jnp.sum(sums[...].astype(f32), axis=0)
    lines = split_rows(join_rows(total, 32)) + split_rows(join_rows(total, 35))
    row = lax.broadcasted_iota(jnp.int32, (16, 128), 0)
    tail = jnp.zeros((16, 128), f32)
    for i, line in enumerate(lines):
        tail = jnp.where(row == i, line, tail)
    out[:, :32, :] = jnp.broadcast_to(total[:32].astype(bf16)[None], (16, 32, 128))
    out[:, 32:, :] = jnp.broadcast_to(tail.astype(bf16)[None], (16, 16, 128))


def add_call(sums):
    return pl.pallas_call(
        add_kernel,
        in_specs=[VMEM],
        out_specs=VMEM,
        out_shape=jax.ShapeDtypeStruct((16, 48, 128), bf16),
        compiler_params=params,
        name="add",
    )(sums)


def update_kernel(sums, state, scaled, out, loss):
    total = jnp.sum(sums[...].astype(f32), axis=0)
    column_new = decay_rate * state[...] + (1.0 - decay_rate) * (total[:16] / V)
    column_scale = lax.rsqrt(column_new)
    row_mean = jnp.broadcast_to(jnp.sum(join_rows(total, 32), keepdims=True) / V, (16, 128))
    square_total = jnp.sum(total[16:32] * column_scale * column_scale, keepdims=True)
    square_total = row_mean * jnp.broadcast_to(square_total, (16, 128))
    update_rms = jnp.sqrt(square_total / (V * D))
    factor = jnp.sqrt(row_mean) * column_scale / jnp.maximum(1.0, update_rms / clip_limit)
    for j in range(16):
        out[j] = (scaled[:OWN, 128 * j : 128 * j + 128] * factor[j : j + 1, :]).astype(bf16)
    loss[...] = jnp.broadcast_to(jnp.sum(join_rows(total, 35), keepdims=True), (8, 128))


def update_call(sums, state, scaled):
    return pl.pallas_call(
        update_kernel,
        in_specs=[VMEM] * 3,
        out_specs=[VMEM] * 2,
        out_shape=[
            jax.ShapeDtypeStruct((16, OWN, 128), bf16),
            jax.ShapeDtypeStruct((8, 128), f32),
        ],
        compiler_params=params,
        name="update",
    )(sums, state, scaled)


def per_device(hidden, head_weight, targets, segments, loss_mask, row_state, column_state):
    core = lax.axis_index("core")
    chip = lax.axis_index(CHIPS)
    odd = lax.axis_index("z") % 2
    chip_start = chip * CHIP_ROWS
    place = jnp.stack([core, lax.axis_index(MP) * VOC + chip_start, odd]).astype(jnp.int32)
    own_state = lax.dynamic_slice_in_dim(row_state, chip_start + core * OWN, OWN, axis=0)
    own_state = jnp.concatenate([own_state, jnp.ones((PAD - OWN,), f32)]).reshape(PAD, 1)
    place, own_state, targets = lax.optimization_barrier((place, own_state, targets))

    first = lax.dynamic_slice_in_dim(hidden, odd * STEP, STEP, axis=1)
    first = trade(jnp.broadcast_to(first[None], (PEERS, TOK, STEP)), CHIPS)
    last = pack(hidden, head_weight, targets, segments, loss_mask, column_state)
    last, first = lax.optimization_barrier((last, first))
    last = trade(last, CHIPS)
    near = lax.ppermute(first[:4], "z", [(i, i ^ 1) for i in range(16)])
    far = lax.ppermute(first[4:], "z", [(i, (i + 1 if i % 2 else i - 1) % 16) for i in range(16)])
    head_other = swap_cores(last[:, TOK:, :])
    hidden_own, partial = half_call(place, first, near, far, last)
    logits, stats, tokens, state = logits_call(place, hidden_own, partial, last, head_other)
    stats, hidden_own = lax.optimization_barrier((stats, hidden_own))
    hidden_other = swap_cores(hidden_own)
    stats = merge_call(trade(stats, PLANE))
    stats = trade(stats, "z")
    score_away, totals = away_call(place, stats, logits, tokens)
    score_other = swap_cores(score_away)
    partial = own_call(place, totals, logits, tokens, hidden_own)
    scaled, sums = grad_call(
        place, partial, score_other, hidden_other, own_state, totals, tokens
    )
    sums = add_call(trade(sums, ("y", "xh", "core", "xl")))
    update, loss = update_call(trade(sums, "z"), state, scaled)
    update_step = trade(update, DP).reshape(VOC, COLS)
    return (update_step, loss[0, 0])


def solution(mesh):
    fine = Mesh(mesh.devices.reshape(4, 2, 2, 16, 2), AXES)
    return jax.shard_map(
        per_device,
        mesh=fine,
        in_specs=(P(DP, None), P(MP, DP), P(DP), P(DP), P(DP), P(MP), P(DP)),
        out_specs=(P(MP, DP), P()),
        check_vma=False,
    )
```

```python
import jax
import jax.numpy as jnp
from jax import lax
from jax.experimental import pallas as pl
from jax.experimental.pallas import tpu as pltpu
from jax.sharding import Mesh, PartitionSpec as P

D = 2048
V = 126976

penalty = 0.25
decay_rate = 1.0 - 16.0 ** (-0.8)
clip_limit = 1.0

AXES = ("y", "xh", "core", "z", "xl")
DP = ("y", "xh", "core")
MP = ("z", "xl")
CHIPS = ("y", "xh")
PLANE = ("y", "xh", "xl")

PEERS = 8
TOK = 128
COLS = 128
VOC = 3968
CHIP_ROWS = 496
OWN = 248
PAD = 256
TOKENS = 1024
SEGS = 64
STEP = 6 * 128
LAST = 4 * 128
f32 = jnp.float32
bf16 = jnp.bfloat16

params = pltpu.CompilerParams(vmem_limit_bytes=16 * 1024 * 1024)
large = pltpu.CompilerParams(vmem_limit_bytes=16 * 1024 * 1024)
VMEM = pl.BlockSpec(memory_space=pltpu.VMEM)
SMEM = pl.BlockSpec(memory_space=pltpu.SMEM)
ANY = pl.BlockSpec(memory_space=pl.ANY)
HBM = pl.BlockSpec(memory_space=pltpu.HBM)


def swap_cores(value):
    return lax.ppermute(value, "core", [(0, 1), (1, 0)])


def trade(value, axes):
    return lax.all_to_all(value, axes, 0, 0)


def pack_kernel(hidden, head, targets, segments, mask, state, out):
    out[0, :TOK, :] = hidden[...]
    for block in range(4):
        height = min(128, CHIP_ROWS - 128 * block)
        out[0, TOK : TOK + height, 128 * block : 128 * block + 128] = head[
            128 * block : 128 * block + height, :
        ]
    row = lax.broadcasted_iota(jnp.int32, (16, 128), 0)
    goal = targets[...]
    value = state[...]
    high = value.astype(bf16).astype(f32)
    rest = value - high
    middle = rest.astype(bf16).astype(f32)
    facts = jnp.zeros((16, 128), f32)
    for place, fact in enumerate(
        [
            (goal >> 16).astype(f32),
            ((goal >> 8) & 255).astype(f32),
            (goal & 255).astype(f32),
            segments[...].astype(f32),
            mask[...].astype(f32),
            high,
            middle,
            rest - middle,
        ]
    ):
        facts = jnp.where(row == place, fact, facts)
    out[0, 2 * TOK - 16 :, LAST - 128 :] = facts.astype(bf16)


def pack(hidden, head, targets, segments, mask, state):
    small = pl.BlockSpec((1, 128), lambda i: (0, 0))
    return pl.pallas_call(
        pack_kernel,
        grid=(PEERS,),
        in_specs=[
            pl.BlockSpec((TOK, LAST), lambda i: (0, 3)),
            pl.BlockSpec((CHIP_ROWS, COLS), lambda i: (i, 0)),
            small,
            small,
            small,
            small,
        ],
        out_specs=pl.BlockSpec((1, 2 * TOK, LAST), lambda i: (i, 0, 0)),
        out_shape=pltpu.HBM((PEERS, 2 * TOK, LAST), bf16),
        compiler_params=large,
        name="pack",
    )(hidden, head, *[x.reshape(1, 128) for x in (targets, segments, mask, state)])


def spread_kernel(hidden, out, part, sems):
    start = pl.multiple_of((lax.axis_index("z") % 2) * STEP, STEP)
    copy = pltpu.make_async_copy(hidden.at[:, pl.ds(start, STEP)], part, sems.at[PEERS])
    copy.start()
    copy.wait()
    copies = [pltpu.make_async_copy(part, out.at[q], sems.at[q]) for q in range(PEERS)]
    for copy in copies:
        copy.start()
    for copy in copies:
        copy.wait()


def spread(hidden):
    return pl.pallas_call(
        spread_kernel,
        in_specs=[HBM],
        out_specs=ANY,
        out_shape=pltpu.HBM((PEERS, TOK, STEP), bf16),
        scratch_shapes=[
            pltpu.VMEM((TOK, STEP), bf16),
            pltpu.SemaphoreType.DMA((PEERS + 1,)),
        ],
        compiler_params=params,
        name="spread",
    )(hidden)


def gather_weight(source, q, rows, weight):
    for block in range(4):
        height = min(128, CHIP_ROWS - 128 * block)
        weight[128 * block : 128 * block + height, q * 128 : q * 128 + 128] = source[
            q, rows : rows + height, 128 * block : 128 * block + 128
        ]


def half_kernel(
    place, first, near, far, last, hidden, sent, partial, facts, weight, beside, rest, sems
):
    core = place[0]
    odd = place[2]
    rest_copies = [
        pltpu.make_async_copy(last.at[q], rest.at[q], sems.at[q]) for q in range(PEERS)
    ]
    beside_copies = [
        pltpu.make_async_copy(
            (near if q < 4 else far).at[q % 4], beside.at[q], sems.at[PEERS + q]
        )
        for q in range(PEERS)
    ]
    for copy in rest_copies + beside_copies:
        copy.start()

    def fill(source, q, start, count):
        for i in range(count):
            column = start + i // 2 + 8 * (core if i % 2 == 0 else 1 - core)
            hidden[q * TOK : q * TOK + TOK, pl.ds(pl.multiple_of(column * 128, 128), 128)] = (
                source[q, :TOK, 128 * i : 128 * i + 128]
            )

    for q in range(PEERS):
        fill(first, q, 3 * odd, 6)
    for q in range(PEERS):
        rest_copies[q].wait()
        fill(rest, q, 6, 4)
        gather_weight(rest, q, TOK, weight)
    facts[...] = rest[:, 2 * TOK - 16 :, LAST - 128 :]
    sent_copies = []
    for q in range(PEERS):
        beside_copies[q].wait()
        fill(beside, q, 3 - 3 * odd, 6)
        if q % 2 == 1:
            tokens = slice((q - 1) * TOK, (q + 1) * TOK)
            copy = pltpu.make_async_copy(
                hidden.at[tokens], sent.at[tokens], sems.at[2 * PEERS + q // 2]
            )
            copy.start()
            sent_copies.append(copy)
            partial[:, tokens] = lax.dot_general(
                weight[...],
                hidden[tokens, : D // 2],
                (((1,), (1,)), ((), ())),
                preferred_element_type=f32,
            )
    for copy in sent_copies:
        copy.wait()


def half_call(place, first, near, far, last):
    return pl.pallas_call(
        half_kernel,
        in_specs=[SMEM, VMEM, ANY, ANY, ANY],
        out_specs=[VMEM, HBM, VMEM, VMEM],
        out_shape=[
            jax.ShapeDtypeStruct((TOKENS, D), bf16),
            pltpu.HBM((TOKENS, D), bf16),
            jax.ShapeDtypeStruct((CHIP_ROWS, TOKENS), f32),
            jax.ShapeDtypeStruct((PEERS, 16, 128), bf16),
        ],
        scratch_shapes=[
            pltpu.VMEM((CHIP_ROWS, D // 2), bf16),
            pltpu.VMEM((PEERS, TOK, STEP), bf16),
            pltpu.VMEM((PEERS, 2 * TOK, LAST), bf16),
            pltpu.SemaphoreType.DMA((2 * PEERS + 4,)),
        ],
        compiler_params=params,
        cost_estimate=pl.CostEstimate(
            flops=10**11, bytes_accessed=10**8, transcendentals=0
        ),
        name="half",
    )(place, first, near, far, last)


def logits_kernel(hidden, partial, other, logits, stats, facts, weight, table):
    facts[...] = other[:, TOK - 16 :, LAST - 128 :]
    for q in range(PEERS):
        gather_weight(other, q, 0, weight)
    logits[CHIP_ROWS:, :] = jnp.zeros((8, TOKENS), f32)
    for block in range(4):
        tokens = slice(256 * block, 256 * block + 256)
        scores = partial[:, tokens] + lax.dot_general(
            weight[...],
            hidden[tokens, D // 2 :],
            (((1,), (1,)), ((), ())),
            preferred_element_type=f32,
        )
        logits[:CHIP_ROWS, tokens] = scores
        for half in range(2):
            part = scores[:, half * 128 : half * 128 + 128]
            q = block * 2 + half
            top = jnp.max(part, axis=0, keepdims=True)
            shifted = jnp.exp(part - top)
            exp_sum = jnp.sum(shifted, axis=0, keepdims=True)
            exp_dot = jnp.sum(shifted * part, axis=0, keepdims=True)
            table[q : q + 1, :] = top + jnp.log(exp_sum)
            table[8 + q : 9 + q, :] = exp_dot / exp_sum
    stats[...] = jnp.broadcast_to(table[...][None], (16, 16, 128))


def logits_call(hidden, partial, other):
    return pl.pallas_call(
        logits_kernel,
        in_specs=[VMEM] * 3,
        out_specs=[VMEM] * 3,
        out_shape=[
            jax.ShapeDtypeStruct((CHIP_ROWS + 8, TOKENS), f32),
            jax.ShapeDtypeStruct((16, 16, 128), f32),
            jax.ShapeDtypeStruct((PEERS, 16, 128), bf16),
        ],
        scratch_shapes=[
            pltpu.VMEM((CHIP_ROWS, D // 2), bf16),
            pltpu.VMEM((16, 128), f32),
        ],
        compiler_params=params,
        name="logits",
    )(hidden, partial, other)


def tokens_kernel(place, own_facts, other_facts, logits, tokens, state, facts):
    core = place[0]
    for q in range(PEERS):
        facts[2 * q + core] = own_facts[q].astype(f32)
        facts[2 * q + 1 - core] = other_facts[q].astype(f32)
    seg = lax.broadcasted_iota(jnp.int32, (SEGS, 128), 0).astype(f32)
    total = jnp.zeros((SEGS, 128), f32)
    for j in range(2 * PEERS):
        total = total + jnp.where(facts[j, 3:4, :] == seg, facts[j, 4:5, :], 0.0)
        state[j : j + 1, :] = facts[j, 5:6, :] + facts[j, 6:7, :] + facts[j, 7:8, :]
    counts = jnp.broadcast_to(jnp.sum(total, axis=1, keepdims=True), (SEGS, 128))
    row = lax.broadcasted_iota(jnp.int32, (CHIP_ROWS, 128), 0) + place[1]
    tokens[...] = jnp.zeros_like(tokens)
    for q in range(PEERS):
        lanes = slice(q * 128, q * 128 + 128)
        fact = facts[2 * q + core]
        goal = fact[0:1] * 65536.0 + fact[1:2] * 256.0 + fact[2:3]
        hit = row == goal.astype(jnp.int32)
        target_logit = jnp.sum(
            jnp.where(hit, logits[:CHIP_ROWS, lanes], 0.0), axis=0, keepdims=True
        )
        own_count = jnp.sum(jnp.where(fact[3:4] == seg, counts, 0.0), axis=0, keepdims=True)
        tok_weight = fact[4:5] / jnp.maximum(own_count, 1.0) / SEGS
        tokens[0:1, lanes] = tok_weight
        tokens[1:2, lanes] = goal
        tokens[2:3, lanes] = tok_weight * target_logit


def tokens_call(place, own_facts, other_facts, logits):
    return pl.pallas_call(
        tokens_kernel,
        in_specs=[SMEM] + [VMEM] * 3,
        out_specs=[VMEM] * 2,
        out_shape=[
            jax.ShapeDtypeStruct((8, TOKENS), f32),
            jax.ShapeDtypeStruct((16, 128), f32),
        ],
        scratch_shapes=[pltpu.VMEM((16, 16, 128), f32)],
        compiler_params=params,
        cost_estimate=pl.CostEstimate(
            flops=10**10, bytes_accessed=10**7, transcendentals=0
        ),
        name="tokens",
    )(place, own_facts, other_facts, logits)


def merged(stats):
    part, mean = stats[:, :8, :], stats[:, 8:, :]
    top = jnp.max(part, axis=0)
    share = jnp.exp(part - top[None])
    total = jnp.sum(share, axis=0)
    return top + jnp.log(total), jnp.sum(share * mean, axis=0) / total


def merge_kernel(stats, out):
    log_total, mean = merged(stats[...])
    out[:, :8, :] = jnp.broadcast_to(log_total[None], (16, 8, 128))
    out[:, 8:, :] = jnp.broadcast_to(mean[None], (16, 8, 128))


def merge_call(stats):
    return pl.pallas_call(
        merge_kernel,
        in_specs=[VMEM],
        out_specs=VMEM,
        out_shape=jax.ShapeDtypeStruct((16, 16, 128), f32),
        compiler_params=params,
        name="merge",
    )(stats)


def score_block(logits, tokens, log_total, entropy, base, row_start, q):
    lanes = slice(q * 128, q * 128 + 128)
    part = logits[pl.ds(pl.multiple_of(base, 8), PAD), lanes]
    row = lax.broadcasted_iota(jnp.int32, (PAD, 128), 0)
    tok_weight = tokens[0:1, lanes]
    goal = tokens[1:2, lanes].astype(jnp.int32)
    hit = (row + (row_start + base) == goal).astype(f32)
    above = part - log_total[q : q + 1, :]
    probability = jnp.exp(above)
    score = tok_weight * (
        probability - hit + penalty * probability * (above + entropy[q : q + 1, :])
    )
    return jnp.where(row < OWN, score, 0.0).astype(bf16)


def fetch(source, target, sems):
    copies = []
    for block in range(4):
        tokens = slice(block * 256, block * 256 + 256)
        copy = pltpu.make_async_copy(source.at[tokens], target.at[tokens], sems.at[block])
        copy.start()
        copies.append(copy)
    return copies


def away_kernel(place, stats, logits, tokens, hidden, score, totals, fetched, sems):
    copies = fetch(hidden, fetched, sems)
    core = place[0]
    log_total, mean = merged(stats[...])
    entropy = log_total - mean
    totals[:8, :] = log_total
    totals[8:, :] = entropy
    for q in range(PEERS):
        score[:, q * 128 : q * 128 + 128] = score_block(
            logits, tokens, log_total, entropy, (1 - core) * OWN, place[1], q
        )
    for copy in copies:
        copy.wait()


def away_call(place, stats, logits, tokens, hidden):
    return pl.pallas_call(
        away_kernel,
        in_specs=[SMEM, VMEM, VMEM, VMEM, HBM],
        out_specs=[VMEM] * 3,
        out_shape=[
            jax.ShapeDtypeStruct((PAD, TOKENS), bf16),
            jax.ShapeDtypeStruct((16, 128), f32),
            pltpu.VMEM((TOKENS, D), bf16),
        ],
        scratch_shapes=[pltpu.SemaphoreType.DMA((4,))],
        compiler_params=params,
        name="away",
    )(place, stats, logits, tokens, hidden)


def own_kernel(place, totals, logits, tokens, hidden, other, out, fetched, score, sems):
    copies = fetch(other, fetched, sems)
    for q in range(PEERS):
        score[:, q * 128 : q * 128 + 128] = score_block(
            logits, tokens, totals[:8, :], totals[8:, :], place[0] * OWN, place[1], q
        )
    for block in range(4):
        lanes = slice(block * 512, block * 512 + 512)
        out[:, lanes] = jnp.dot(score[...], hidden[:, lanes], preferred_element_type=f32)
    for copy in copies:
        copy.wait()


def own_call(place, totals, logits, tokens, hidden, other):
    return pl.pallas_call(
        own_kernel,
        in_specs=[SMEM] + [VMEM] * 4 + [HBM],
        out_specs=[VMEM] * 2,
        out_shape=[
            jax.ShapeDtypeStruct((PAD, D), f32),
            pltpu.VMEM((TOKENS, D), bf16),
        ],
        scratch_shapes=[
            pltpu.VMEM((PAD, TOKENS), bf16),
            pltpu.SemaphoreType.DMA((4,)),
        ],
        compiler_params=params,
        name="own",
    )(place, totals, logits, tokens, hidden, other)


def split_rows(value):
    high = value.astype(bf16).astype(f32)
    rest = value - high
    middle = rest.astype(bf16).astype(f32)
    return [high, middle, rest - middle]


def join_rows(total, start):
    return total[start : start + 1] + total[start + 1 : start + 2] + total[start + 2 : start + 3]


def grad_kernel(
    place, partial, score, hidden, state, totals, tokens, scaled, sums, grad, table
):
    core = place[0]
    places = [2 * i + core for i in range(8)] + [2 * i + 1 - core for i in range(8)]
    squares = jnp.zeros((PAD, 128), f32)
    for source in range(4):
        block = (source + 2) % 4
        lanes = slice(block * 512, block * 512 + 512)
        start = source * 512
        value = partial[:, lanes] + jnp.dot(
            score[...], hidden[:, start : start + 512], preferred_element_type=f32
        )
        grad[:, lanes] = value
        for i in range(4):
            part = value[:, 128 * i : 128 * i + 128]
            part = part * part
            squares = squares + part
            table[pl.ds(places[4 * block + i], 1), :] = jnp.sum(part, axis=0, keepdims=True)
    diagonal = lax.broadcasted_iota(jnp.int32, (PAD, PAD), 0) == lax.broadcasted_iota(
        jnp.int32, (PAD, PAD), 1
    )
    old = jnp.sum(jnp.where(diagonal, state[...], 0.0), axis=1, keepdims=True)
    row_new = decay_rate * old + (1.0 - decay_rate) * (
        jnp.sum(squares, axis=1, keepdims=True) / D
    )
    scale = jnp.broadcast_to(lax.rsqrt(row_new), (PAD, 128))
    row = lax.broadcasted_iota(jnp.int32, (PAD, 128), 0)
    lane = lax.broadcasted_iota(jnp.int32, (PAD, 128), 1)
    kept = jnp.where((row < OWN) & (lane == 0), jnp.broadcast_to(row_new, (PAD, 128)), 0.0)
    row_total = jnp.sum(kept, axis=0, keepdims=True)
    loss = jnp.zeros((1, 128), f32)
    for q in range(PEERS):
        lanes = slice(128 * q, 128 * q + 128)
        loss = loss + (
            tokens[0:1, lanes]
            * (totals[q : q + 1, :] - penalty * totals[8 + q : 9 + q, :])
            * (1.0 / 256.0)
            - tokens[2:3, lanes]
        )
    table[32:48, :] = jnp.zeros((16, 128), f32)
    for i, line in enumerate(split_rows(row_total) + split_rows(loss)):
        table[32 + i : 33 + i, :] = line
    for i, j in enumerate(places):
        part = grad[:, 128 * i : 128 * i + 128] * scale
        scaled[:, pl.ds(pl.multiple_of(j * 128, 128), 128)] = part
        table[pl.ds(16 + j, 1), :] = jnp.sum(part * part, axis=0, keepdims=True)
    sums[...] = jnp.broadcast_to(table[...].astype(bf16)[None], (32, 48, 128))


def grad_call(place, partial, score, hidden, state, totals, tokens):
    return pl.pallas_call(
        grad_kernel,
        in_specs=[SMEM] + [VMEM] * 6,
        out_specs=[VMEM] * 2,
        out_shape=[
            jax.ShapeDtypeStruct((PAD, D), f32),
            jax.ShapeDtypeStruct((32, 48, 128), bf16),
        ],
        scratch_shapes=[
            pltpu.VMEM((PAD, D), f32),
            pltpu.VMEM((48, 128), f32),
        ],
        compiler_params=params,
        name="grad",
    )(place, partial, score, hidden, state, totals, tokens)


def add_kernel(sums, out):
    total = jnp.sum(sums[...].astype(f32), axis=0)
    lines = split_rows(join_rows(total, 32)) + split_rows(join_rows(total, 35))
    row = lax.broadcasted_iota(jnp.int32, (16, 128), 0)
    tail = jnp.zeros((16, 128), f32)
    for i, line in enumerate(lines):
        tail = jnp.where(row == i, line, tail)
    out[:, :32, :] = jnp.broadcast_to(total[:32].astype(bf16)[None], (16, 32, 128))
    out[:, 32:, :] = jnp.broadcast_to(tail.astype(bf16)[None], (16, 16, 128))


def add_call(sums):
    return pl.pallas_call(
        add_kernel,
        in_specs=[VMEM],
        out_specs=VMEM,
        out_shape=jax.ShapeDtypeStruct((16, 48, 128), bf16),
        compiler_params=params,
        name="add",
    )(sums)


def update_kernel(sums, state, scaled, out, loss):
    total = jnp.sum(sums[...].astype(f32), axis=0)
    column_new = decay_rate * state[...] + (1.0 - decay_rate) * (total[:16] / V)
    column_scale = lax.rsqrt(column_new)
    row_mean = jnp.broadcast_to(jnp.sum(join_rows(total, 32), keepdims=True) / V, (16, 128))
    square_total = jnp.sum(total[16:32] * column_scale * column_scale, keepdims=True)
    square_total = row_mean * jnp.broadcast_to(square_total, (16, 128))
    update_rms = jnp.sqrt(square_total / (V * D))
    factor = jnp.sqrt(row_mean) * column_scale / jnp.maximum(1.0, update_rms / clip_limit)
    for j in range(16):
        out[j] = (scaled[:OWN, 128 * j : 128 * j + 128] * factor[j : j + 1, :]).astype(bf16)
    loss[...] = jnp.broadcast_to(jnp.sum(join_rows(total, 35), keepdims=True), (8, 128))


def update_call(sums, state, scaled):
    return pl.pallas_call(
        update_kernel,
        in_specs=[VMEM] * 3,
        out_specs=[VMEM] * 2,
        out_shape=[
            jax.ShapeDtypeStruct((16, OWN, 128), bf16),
            jax.ShapeDtypeStruct((8, 128), f32),
        ],
        compiler_params=params,
        name="update",
    )(sums, state, scaled)


def per_device(hidden, head_weight, targets, segments, loss_mask, row_state, column_state):
    core = lax.axis_index("core")
    chip = lax.axis_index(CHIPS)
    odd = lax.axis_index("z") % 2
    chip_start = chip * CHIP_ROWS
    place = jnp.stack([core, lax.axis_index(MP) * VOC + chip_start, odd]).astype(jnp.int32)
    own_state = lax.dynamic_slice_in_dim(row_state, chip_start + core * OWN, OWN, axis=0)
    own_state = jnp.concatenate([own_state, jnp.ones((PAD - OWN,), f32)]).reshape(1, PAD)
    place, own_state, targets = lax.optimization_barrier((place, own_state, targets))

    first = trade(spread(hidden), CHIPS)
    last = pack(hidden, head_weight, targets, segments, loss_mask, column_state)
    last, first = lax.optimization_barrier((last, first))
    last = trade(last, CHIPS)
    near = lax.ppermute(first[:4], "z", [(i, i ^ 1) for i in range(16)])
    far = lax.ppermute(first[4:], "z", [(i, (i + 1 if i % 2 else i - 1) % 16) for i in range(16)])
    head_other = swap_cores(last[:, TOK:, :])
    hidden_own, hidden_sent, partial, own_facts = half_call(place, first, near, far, last)
    logits, stats, other_facts = logits_call(hidden_own, partial, head_other)
    stats, hidden_sent = lax.optimization_barrier((stats, hidden_sent))
    tokens, state = tokens_call(place, own_facts, other_facts, logits)
    hidden_other = swap_cores(hidden_sent)
    stats = merge_call(trade(stats, PLANE))
    stats = trade(stats, "z")
    score_away, totals, hidden_own = away_call(place, stats, logits, tokens, hidden_sent)
    score_other = swap_cores(score_away)
    partial, hidden_other = own_call(
        place, totals, logits, tokens, hidden_own, hidden_other
    )
    scaled, sums = grad_call(
        place, partial, score_other, hidden_other, own_state, totals, tokens
    )
    sums = add_call(trade(sums, ("y", "xh", "core", "xl")))
    update, loss = update_call(trade(sums, "z"), state, scaled)
    update_step = trade(update, DP).reshape(VOC, COLS)
    return (update_step, loss[0, 0])


def solution(mesh):
    fine = Mesh(mesh.devices.reshape(4, 2, 2, 16, 2), AXES)
    return jax.shard_map(
        per_device,
        mesh=fine,
        in_specs=(P(DP, None), P(MP, DP), P(DP), P(DP), P(DP), P(MP), P(DP)),
        out_specs=(P(MP, DP), P()),
        check_vma=False,
    )
```

```python
import jax
import jax.numpy as jnp
from jax import lax
from jax.experimental import pallas as pl
from jax.experimental.pallas import tpu as pltpu
from jax.sharding import Mesh, PartitionSpec as P

D = 2048
V = 126976

penalty = 0.25
decay_rate = 1.0 - 16.0 ** (-0.8)
clip_limit = 1.0

AXES = ("y", "xh", "core", "z", "xl")
DP = ("y", "xh", "core")
MP = ("z", "xl")
CHIPS = ("y", "xh")
PLANE = ("y", "xh", "xl")

PEERS = 8
TOK = 128
COLS = 128
VOC = 3968
CHIP_ROWS = 496
OWN = 248
PAD = 256
TOKENS = 1024
SEGS = 64
STEP = 6 * 128
LAST = 4 * 128
f32 = jnp.float32
bf16 = jnp.bfloat16

params = pltpu.CompilerParams(vmem_limit_bytes=16 * 1024 * 1024)
large = pltpu.CompilerParams(vmem_limit_bytes=63 * 1024 * 1024 + 512 * 1024)
VMEM = pl.BlockSpec(memory_space=pltpu.VMEM)
SMEM = pl.BlockSpec(memory_space=pltpu.SMEM)
ANY = pl.BlockSpec(memory_space=pl.ANY)
HBM = pl.BlockSpec(memory_space=pltpu.HBM)


def swap_cores(value):
    return lax.ppermute(value, "core", [(0, 1), (1, 0)])


def trade(value, axes):
    return lax.all_to_all(value, axes, 0, 0)


def pack_kernel(hidden, head, targets, segments, mask, state, out):
    out[0, :TOK, :] = hidden[...]
    for block in range(4):
        height = min(128, CHIP_ROWS - 128 * block)
        out[0, TOK : TOK + height, 128 * block : 128 * block + 128] = head[
            128 * block : 128 * block + height, :
        ]
    row = lax.broadcasted_iota(jnp.int32, (16, 128), 0)
    goal = targets[...]
    value = state[...]
    high = value.astype(bf16).astype(f32)
    rest = value - high
    middle = rest.astype(bf16).astype(f32)
    facts = jnp.zeros((16, 128), f32)
    for place, fact in enumerate(
        [
            (goal >> 16).astype(f32),
            ((goal >> 8) & 255).astype(f32),
            (goal & 255).astype(f32),
            segments[...].astype(f32),
            mask[...].astype(f32),
            high,
            middle,
            rest - middle,
        ]
    ):
        facts = jnp.where(row == place, fact, facts)
    out[0, 2 * TOK - 16 :, LAST - 128 :] = facts.astype(bf16)


def pack(hidden, head, targets, segments, mask, state):
    small = pl.BlockSpec((1, 128), lambda i: (0, 0))
    return pl.pallas_call(
        pack_kernel,
        grid=(PEERS,),
        in_specs=[
            pl.BlockSpec((TOK, LAST), lambda i: (0, 3)),
            pl.BlockSpec((CHIP_ROWS, COLS), lambda i: (i, 0)),
            small,
            small,
            small,
            small,
        ],
        out_specs=pl.BlockSpec((1, 2 * TOK, LAST), lambda i: (i, 0, 0)),
        out_shape=pltpu.HBM((PEERS, 2 * TOK, LAST), bf16),
        compiler_params=params,
        name="pack",
    )(hidden, head, *[x.reshape(1, 128) for x in (targets, segments, mask, state)])


def spread_kernel(hidden, out, part, sems):
    start = pl.multiple_of((lax.axis_index("z") % 2) * STEP, STEP)
    copy = pltpu.make_async_copy(hidden.at[:, pl.ds(start, STEP)], part, sems.at[PEERS])
    copy.start()
    copy.wait()
    copies = [pltpu.make_async_copy(part, out.at[q], sems.at[q]) for q in range(PEERS)]
    for copy in copies:
        copy.start()
    for copy in copies:
        copy.wait()


def spread(hidden):
    return pl.pallas_call(
        spread_kernel,
        in_specs=[HBM],
        out_specs=ANY,
        out_shape=pltpu.HBM((PEERS, TOK, STEP), bf16),
        scratch_shapes=[
            pltpu.VMEM((TOK, STEP), bf16),
            pltpu.SemaphoreType.DMA((PEERS + 1,)),
        ],
        compiler_params=large,
        name="spread",
    )(hidden)


def gather_weight(source, q, rows, weight):
    for block in range(4):
        height = min(128, CHIP_ROWS - 128 * block)
        weight[128 * block : 128 * block + height, q * 128 : q * 128 + 128] = source[
            q, rows : rows + height, 128 * block : 128 * block + 128
        ]


def half_kernel(
    place, first, near, far, last, hidden, sent, partial, facts, weight, beside, rest, sems
):
    core = place[0]
    odd = place[2]
    rest_copies = [
        pltpu.make_async_copy(last.at[q], rest.at[q], sems.at[q]) for q in range(PEERS)
    ]
    beside_copies = [
        pltpu.make_async_copy(
            (near if q < 4 else far).at[q % 4], beside.at[q], sems.at[PEERS + q]
        )
        for q in range(PEERS)
    ]
    for q in range(PEERS):
        rest_copies[q].start()
        beside_copies[q].start()

    def fill(source, q, start, count):
        for i in range(count):
            column = start + i // 2 + 8 * (core if i % 2 == 0 else 1 - core)
            hidden[q * TOK : q * TOK + TOK, pl.ds(pl.multiple_of(column * 128, 128), 128)] = (
                source[q, :TOK, 128 * i : 128 * i + 128]
            )

    sent_copies = []
    for q in range(PEERS):
        fill(first, q, 3 * odd, 6)
        rest_copies[q].wait()
        fill(rest, q, 6, 4)
        gather_weight(rest, q, TOK, weight)
        beside_copies[q].wait()
        fill(beside, q, 3 - 3 * odd, 6)
        if q % 2 == 1:
            tokens = slice((q - 1) * TOK, (q + 1) * TOK)
            copy = pltpu.make_async_copy(
                hidden.at[tokens], sent.at[tokens], sems.at[2 * PEERS + q // 2]
            )
            copy.start()
            sent_copies.append(copy)
    facts[...] = rest[:, 2 * TOK - 16 :, LAST - 128 :]
    for block in range(4):
        tokens = slice(256 * block, 256 * block + 256)
        partial[:, tokens] = lax.dot_general(
            weight[...],
            hidden[tokens, : D // 2],
            (((1,), (1,)), ((), ())),
            preferred_element_type=f32,
        )
    for copy in sent_copies:
        copy.wait()


def half_call(place, first, near, far, last):
    return pl.pallas_call(
        half_kernel,
        in_specs=[SMEM, VMEM, ANY, ANY, ANY],
        out_specs=[VMEM, HBM, VMEM, VMEM],
        out_shape=[
            jax.ShapeDtypeStruct((TOKENS, D), bf16),
            pltpu.HBM((TOKENS, D), bf16),
            jax.ShapeDtypeStruct((CHIP_ROWS, TOKENS), f32),
            jax.ShapeDtypeStruct((PEERS, 16, 128), bf16),
        ],
        scratch_shapes=[
            pltpu.VMEM((CHIP_ROWS, D // 2), bf16),
            pltpu.VMEM((PEERS, TOK, STEP), bf16),
            pltpu.VMEM((PEERS, 2 * TOK, LAST), bf16),
            pltpu.SemaphoreType.DMA((2 * PEERS + 4,)),
        ],
        compiler_params=params,
        cost_estimate=pl.CostEstimate(
            flops=10**11, bytes_accessed=10**8, transcendentals=0
        ),
        name="half",
    )(place, first, near, far, last)


def logits_kernel(hidden, partial, other, logits, stats, facts, weight, table):
    facts[...] = other[:, 2 * TOK - 16 :, LAST - 128 :]
    for q in range(PEERS):
        gather_weight(other, q, TOK, weight)
    logits[CHIP_ROWS:, :] = jnp.zeros((8, TOKENS), f32)
    for block in range(4):
        tokens = slice(256 * block, 256 * block + 256)
        scores = partial[:, tokens] + lax.dot_general(
            weight[...],
            hidden[tokens, D // 2 :],
            (((1,), (1,)), ((), ())),
            preferred_element_type=f32,
        )
        logits[:CHIP_ROWS, tokens] = scores
        for half in range(2):
            part = scores[:, half * 128 : half * 128 + 128]
            q = block * 2 + half
            top = jnp.max(part, axis=0, keepdims=True)
            shifted = jnp.exp(part - top)
            exp_sum = jnp.sum(shifted, axis=0, keepdims=True)
            exp_dot = jnp.sum(shifted * part, axis=0, keepdims=True)
            table[q : q + 1, :] = top + jnp.log(exp_sum)
            table[8 + q : 9 + q, :] = exp_dot / exp_sum
    stats[...] = jnp.broadcast_to(table[...][None], (16, 16, 128))


def logits_call(hidden, partial, other):
    return pl.pallas_call(
        logits_kernel,
        in_specs=[VMEM] * 3,
        out_specs=[VMEM] * 3,
        out_shape=[
            jax.ShapeDtypeStruct((CHIP_ROWS + 8, TOKENS), f32),
            jax.ShapeDtypeStruct((16, 16, 128), f32),
            jax.ShapeDtypeStruct((PEERS, 16, 128), bf16),
        ],
        scratch_shapes=[
            pltpu.VMEM((CHIP_ROWS, D // 2), bf16),
            pltpu.VMEM((16, 128), f32),
        ],
        compiler_params=params,
        name="logits",
    )(hidden, partial, other)


def tokens_kernel(place, own_facts, other_facts, logits, tokens, state, facts):
    core = place[0]
    for q in range(PEERS):
        facts[2 * q + core] = own_facts[q].astype(f32)
        facts[2 * q + 1 - core] = other_facts[q].astype(f32)
    seg = lax.broadcasted_iota(jnp.int32, (SEGS, 128), 0).astype(f32)
    total = jnp.zeros((SEGS, 128), f32)
    for j in range(2 * PEERS):
        total = total + jnp.where(facts[j, 3:4, :] == seg, facts[j, 4:5, :], 0.0)
        state[j : j + 1, :] = facts[j, 5:6, :] + facts[j, 6:7, :] + facts[j, 7:8, :]
    counts = jnp.broadcast_to(jnp.sum(total, axis=1, keepdims=True), (SEGS, 128))
    row = lax.broadcasted_iota(jnp.int32, (CHIP_ROWS, 128), 0) + place[1]
    tokens[...] = jnp.zeros_like(tokens)
    for q in range(PEERS):
        lanes = slice(q * 128, q * 128 + 128)
        fact = facts[2 * q + core]
        goal = fact[0:1] * 65536.0 + fact[1:2] * 256.0 + fact[2:3]
        hit = row == goal.astype(jnp.int32)
        target_logit = jnp.sum(
            jnp.where(hit, logits[:CHIP_ROWS, lanes], 0.0), axis=0, keepdims=True
        )
        own_count = jnp.sum(jnp.where(fact[3:4] == seg, counts, 0.0), axis=0, keepdims=True)
        tok_weight = fact[4:5] / jnp.maximum(own_count, 1.0) / SEGS
        tokens[0:1, lanes] = tok_weight
        tokens[1:2, lanes] = goal
        tokens[2:3, lanes] = tok_weight * target_logit


def tokens_call(place, own_facts, other_facts, logits):
    return pl.pallas_call(
        tokens_kernel,
        in_specs=[SMEM] + [VMEM] * 3,
        out_specs=[VMEM] * 2,
        out_shape=[
            jax.ShapeDtypeStruct((8, TOKENS), f32),
            jax.ShapeDtypeStruct((16, 128), f32),
        ],
        scratch_shapes=[pltpu.VMEM((16, 16, 128), f32)],
        compiler_params=params,
        cost_estimate=pl.CostEstimate(
            flops=10**10, bytes_accessed=10**7, transcendentals=0
        ),
        name="tokens",
    )(place, own_facts, other_facts, logits)


def merged(stats):
    part, mean = stats[:, :8, :], stats[:, 8:, :]
    top = jnp.max(part, axis=0)
    share = jnp.exp(part - top[None])
    total = jnp.sum(share, axis=0)
    return top + jnp.log(total), jnp.sum(share * mean, axis=0) / total


def merge_kernel(stats, out):
    log_total, mean = merged(stats[...])
    out[:, :8, :] = jnp.broadcast_to(log_total[None], (16, 8, 128))
    out[:, 8:, :] = jnp.broadcast_to(mean[None], (16, 8, 128))


def merge_call(stats):
    return pl.pallas_call(
        merge_kernel,
        in_specs=[VMEM],
        out_specs=VMEM,
        out_shape=jax.ShapeDtypeStruct((16, 16, 128), f32),
        compiler_params=params,
        name="merge",
    )(stats)


def score_block(logits, tokens, log_total, entropy, base, row_start, q):
    lanes = slice(q * 128, q * 128 + 128)
    part = logits[pl.ds(pl.multiple_of(base, 8), PAD), lanes]
    row = lax.broadcasted_iota(jnp.int32, (PAD, 128), 0)
    tok_weight = tokens[0:1, lanes]
    goal = tokens[1:2, lanes].astype(jnp.int32)
    hit = (row + (row_start + base) == goal).astype(f32)
    above = part - log_total[q : q + 1, :]
    probability = jnp.exp(above)
    score = tok_weight * (
        probability - hit + penalty * probability * (above + entropy[q : q + 1, :])
    )
    return jnp.where(row < OWN, score, 0.0).astype(bf16)


def fetch(source, target, sems):
    copies = []
    for block in range(4):
        tokens = slice(block * 256, block * 256 + 256)
        copy = pltpu.make_async_copy(source.at[tokens], target.at[tokens], sems.at[block])
        copy.start()
        copies.append(copy)
    return copies


def away_kernel(place, stats, logits, tokens, hidden, score, totals, fetched, sems):
    copies = fetch(hidden, fetched, sems)
    core = place[0]
    log_total, mean = merged(stats[...])
    entropy = log_total - mean
    totals[:8, :] = log_total
    totals[8:, :] = entropy
    for q in range(PEERS):
        score[:, q * 128 : q * 128 + 128] = score_block(
            logits, tokens, log_total, entropy, (1 - core) * OWN, place[1], q
        )
    for copy in copies:
        copy.wait()


def away_call(place, stats, logits, tokens, hidden):
    return pl.pallas_call(
        away_kernel,
        in_specs=[SMEM, VMEM, VMEM, VMEM, HBM],
        out_specs=[VMEM] * 3,
        out_shape=[
            jax.ShapeDtypeStruct((PAD, TOKENS), bf16),
            jax.ShapeDtypeStruct((16, 128), f32),
            pltpu.VMEM((TOKENS, D), bf16),
        ],
        scratch_shapes=[pltpu.SemaphoreType.DMA((4,))],
        compiler_params=params,
        name="away",
    )(place, stats, logits, tokens, hidden)


def own_kernel(place, totals, logits, tokens, hidden, other, out, fetched, score, sems):
    copies = fetch(other, fetched, sems)
    for q in range(PEERS):
        score[:, q * 128 : q * 128 + 128] = score_block(
            logits, tokens, totals[:8, :], totals[8:, :], place[0] * OWN, place[1], q
        )
    for block in range(4):
        lanes = slice(block * 512, block * 512 + 512)
        out[:, lanes] = jnp.dot(score[...], hidden[:, lanes], preferred_element_type=f32)
    for copy in copies:
        copy.wait()


def own_call(place, totals, logits, tokens, hidden, other):
    return pl.pallas_call(
        own_kernel,
        in_specs=[SMEM] + [VMEM] * 4 + [HBM],
        out_specs=[VMEM] * 2,
        out_shape=[
            jax.ShapeDtypeStruct((PAD, D), f32),
            pltpu.VMEM((TOKENS, D), bf16),
        ],
        scratch_shapes=[
            pltpu.VMEM((PAD, TOKENS), bf16),
            pltpu.SemaphoreType.DMA((4,)),
        ],
        compiler_params=params,
        name="own",
    )(place, totals, logits, tokens, hidden, other)


def split_rows(value):
    high = value.astype(bf16).astype(f32)
    rest = value - high
    middle = rest.astype(bf16).astype(f32)
    return [high, middle, rest - middle]


def join_rows(total, start):
    return total[start : start + 1] + total[start + 1 : start + 2] + total[start + 2 : start + 3]


def grad_kernel(
    place, partial, score, hidden, state, totals, tokens, scaled, sums, grad, table
):
    core = place[0]
    places = [2 * i + core for i in range(8)] + [2 * i + 1 - core for i in range(8)]
    squares = jnp.zeros((PAD, 128), f32)
    for source in range(4):
        block = (source + 2) % 4
        lanes = slice(block * 512, block * 512 + 512)
        start = source * 512
        value = partial[:, lanes] + jnp.dot(
            score[...], hidden[:, start : start + 512], preferred_element_type=f32
        )
        grad[:, lanes] = value
        for i in range(4):
            part = value[:, 128 * i : 128 * i + 128]
            part = part * part
            squares = squares + part
            table[pl.ds(places[4 * block + i], 1), :] = jnp.sum(part, axis=0, keepdims=True)
    diagonal = lax.broadcasted_iota(jnp.int32, (PAD, PAD), 0) == lax.broadcasted_iota(
        jnp.int32, (PAD, PAD), 1
    )
    old = jnp.sum(jnp.where(diagonal, state[...], 0.0), axis=1, keepdims=True)
    row_new = decay_rate * old + (1.0 - decay_rate) * (
        jnp.sum(squares, axis=1, keepdims=True) / D
    )
    scale = jnp.broadcast_to(lax.rsqrt(row_new), (PAD, 128))
    row = lax.broadcasted_iota(jnp.int32, (PAD, 128), 0)
    lane = lax.broadcasted_iota(jnp.int32, (PAD, 128), 1)
    kept = jnp.where((row < OWN) & (lane == 0), jnp.broadcast_to(row_new, (PAD, 128)), 0.0)
    row_total = jnp.sum(kept, axis=0, keepdims=True)
    loss = jnp.zeros((1, 128), f32)
    for q in range(PEERS):
        lanes = slice(128 * q, 128 * q + 128)
        loss = loss + (
            tokens[0:1, lanes]
            * (totals[q : q + 1, :] - penalty * totals[8 + q : 9 + q, :])
            * (1.0 / 256.0)
            - tokens[2:3, lanes]
        )
    table[32:48, :] = jnp.zeros((16, 128), f32)
    for i, line in enumerate(split_rows(row_total) + split_rows(loss)):
        table[32 + i : 33 + i, :] = line
    for i, j in enumerate(places):
        part = grad[:, 128 * i : 128 * i + 128] * scale
        scaled[:, pl.ds(pl.multiple_of(j * 128, 128), 128)] = part
        table[pl.ds(16 + j, 1), :] = jnp.sum(part * part, axis=0, keepdims=True)
    sums[...] = jnp.broadcast_to(table[...].astype(bf16)[None], (32, 48, 128))


def grad_call(place, partial, score, hidden, state, totals, tokens):
    return pl.pallas_call(
        grad_kernel,
        in_specs=[SMEM] + [VMEM] * 6,
        out_specs=[VMEM] * 2,
        out_shape=[
            jax.ShapeDtypeStruct((PAD, D), f32),
            jax.ShapeDtypeStruct((32, 48, 128), bf16),
        ],
        scratch_shapes=[
            pltpu.VMEM((PAD, D), f32),
            pltpu.VMEM((48, 128), f32),
        ],
        compiler_params=params,
        name="grad",
    )(place, partial, score, hidden, state, totals, tokens)


def add_kernel(sums, out):
    total = jnp.sum(sums[...].astype(f32), axis=0)
    lines = split_rows(join_rows(total, 32)) + split_rows(join_rows(total, 35))
    row = lax.broadcasted_iota(jnp.int32, (16, 128), 0)
    tail = jnp.zeros((16, 128), f32)
    for i, line in enumerate(lines):
        tail = jnp.where(row == i, line, tail)
    out[:, :32, :] = jnp.broadcast_to(total[:32].astype(bf16)[None], (16, 32, 128))
    out[:, 32:, :] = jnp.broadcast_to(tail.astype(bf16)[None], (16, 16, 128))


def add_call(sums):
    return pl.pallas_call(
        add_kernel,
        in_specs=[VMEM],
        out_specs=VMEM,
        out_shape=jax.ShapeDtypeStruct((16, 48, 128), bf16),
        compiler_params=params,
        name="add",
    )(sums)


def update_kernel(sums, state, scaled, out, loss):
    total = jnp.sum(sums[...].astype(f32), axis=0)
    column_new = decay_rate * state[...] + (1.0 - decay_rate) * (total[:16] / V)
    column_scale = lax.rsqrt(column_new)
    row_mean = jnp.broadcast_to(jnp.sum(join_rows(total, 32), keepdims=True) / V, (16, 128))
    square_total = jnp.sum(total[16:32] * column_scale * column_scale, keepdims=True)
    square_total = row_mean * jnp.broadcast_to(square_total, (16, 128))
    update_rms = jnp.sqrt(square_total / (V * D))
    factor = jnp.sqrt(row_mean) * column_scale / jnp.maximum(1.0, update_rms / clip_limit)
    for j in range(16):
        out[j] = (scaled[:OWN, 128 * j : 128 * j + 128] * factor[j : j + 1, :]).astype(bf16)
    loss[...] = jnp.broadcast_to(jnp.sum(join_rows(total, 35), keepdims=True), (8, 128))


def update_call(sums, state, scaled):
    return pl.pallas_call(
        update_kernel,
        in_specs=[VMEM] * 3,
        out_specs=[VMEM] * 2,
        out_shape=[
            jax.ShapeDtypeStruct((16, OWN, 128), bf16),
            jax.ShapeDtypeStruct((8, 128), f32),
        ],
        compiler_params=params,
        name="update",
    )(sums, state, scaled)


def per_device(hidden, head_weight, targets, segments, loss_mask, row_state, column_state):
    core = lax.axis_index("core")
    chip = lax.axis_index(CHIPS)
    odd = lax.axis_index("z") % 2
    chip_start = chip * CHIP_ROWS
    place = jnp.stack([core, lax.axis_index(MP) * VOC + chip_start, odd]).astype(jnp.int32)
    own_state = lax.dynamic_slice_in_dim(row_state, chip_start + core * OWN, OWN, axis=0)
    own_state = jnp.concatenate([own_state, jnp.ones((PAD - OWN,), f32)]).reshape(1, PAD)
    place, own_state, targets = lax.optimization_barrier((place, own_state, targets))

    first = trade(spread(hidden), CHIPS)
    last = pack(hidden, head_weight, targets, segments, loss_mask, column_state)
    last, first = lax.optimization_barrier((last, first))
    last = trade(last, CHIPS)
    near = lax.ppermute(first[:4], "z", [(i, i ^ 1) for i in range(16)])
    far = lax.ppermute(first[4:], "z", [(i, (i + 1 if i % 2 else i - 1) % 16) for i in range(16)])
    last_other = swap_cores(last)
    hidden_own, hidden_sent, partial, own_facts = half_call(place, first, near, far, last)
    logits, stats, other_facts = logits_call(hidden_own, partial, last_other)
    stats, hidden_sent = lax.optimization_barrier((stats, hidden_sent))
    tokens, state = tokens_call(place, own_facts, other_facts, logits)
    hidden_other = swap_cores(hidden_sent)
    stats = merge_call(trade(stats, PLANE))
    stats = trade(stats, "z")
    score_away, totals, hidden_own = away_call(place, stats, logits, tokens, hidden_sent)
    score_other = swap_cores(score_away)
    partial, hidden_other = own_call(
        place, totals, logits, tokens, hidden_own, hidden_other
    )
    scaled, sums = grad_call(
        place, partial, score_other, hidden_other, own_state, totals, tokens
    )
    sums = add_call(trade(sums, ("y", "xh", "core", "xl")))
    update, loss = update_call(trade(sums, "z"), state, scaled)
    update_step = trade(update, DP).reshape(VOC, COLS)
    return (update_step, loss[0, 0])


def solution(mesh):
    fine = Mesh(mesh.devices.reshape(4, 2, 2, 16, 2), AXES)
    return jax.shard_map(
        per_device,
        mesh=fine,
        in_specs=(P(DP, None), P(MP, DP), P(DP), P(DP), P(DP), P(MP), P(DP)),
        out_specs=(P(MP, DP), P()),
        check_vma=False,
    )
```

```python
import jax
import jax.numpy as jnp
from jax import lax
from jax.experimental import pallas as pl
from jax.experimental.pallas import tpu as pltpu
from jax.sharding import Mesh, PartitionSpec as P

D = 2048
V = 126976

penalty = 0.25
decay_rate = 1.0 - 16.0 ** (-0.8)
clip_limit = 1.0

AXES = ("y", "xh", "core", "z", "xl")
DP = ("y", "xh", "core")
MP = ("z", "xl")
CHIPS = ("y", "xh")
PLANE = ("y", "xh", "xl")

PEERS = 8
TOK = 128
COLS = 128
VOC = 3968
CHIP_ROWS = 496
OWN = 248
PAD = 256
TOKENS = 1024
SEGS = 64
SUMS = 40
STEP = 6 * 128
LAST = 4 * 128
f32 = jnp.float32
bf16 = jnp.bfloat16

params = pltpu.CompilerParams(vmem_limit_bytes=16 * 1024 * 1024)
large = pltpu.CompilerParams(vmem_limit_bytes=63 * 1024 * 1024 + 512 * 1024)
VMEM = pl.BlockSpec(memory_space=pltpu.VMEM)
SMEM = pl.BlockSpec(memory_space=pltpu.SMEM)
ANY = pl.BlockSpec(memory_space=pl.ANY)
HBM = pl.BlockSpec(memory_space=pltpu.HBM)


def swap_cores(value):
    return lax.ppermute(value, "core", [(0, 1), (1, 0)])


def trade(value, axes):
    return lax.all_to_all(value, axes, 0, 0)


def pack_kernel(hidden, head, targets, segments, mask, state, out):
    out[0, :TOK, :] = hidden[...]
    for block in range(4):
        height = min(128, CHIP_ROWS - 128 * block)
        out[0, TOK : TOK + height, 128 * block : 128 * block + 128] = head[
            128 * block : 128 * block + height, :
        ]
    row = lax.broadcasted_iota(jnp.int32, (16, 128), 0)
    goal = targets[...]
    value = state[...]
    high = value.astype(bf16).astype(f32)
    rest = value - high
    middle = rest.astype(bf16).astype(f32)
    facts = jnp.zeros((16, 128), f32)
    for place, fact in enumerate(
        [
            (goal >> 16).astype(f32),
            ((goal >> 8) & 255).astype(f32),
            (goal & 255).astype(f32),
            segments[...].astype(f32),
            mask[...].astype(f32),
            high,
            middle,
            rest - middle,
        ]
    ):
        facts = jnp.where(row == place, fact, facts)
    out[0, 2 * TOK - 16 :, LAST - 128 :] = facts.astype(bf16)


def pack(hidden, head, targets, segments, mask, state):
    small = pl.BlockSpec((1, 128), lambda i: (0, 0))
    return pl.pallas_call(
        pack_kernel,
        grid=(PEERS,),
        in_specs=[
            pl.BlockSpec((TOK, LAST), lambda i: (0, 3)),
            pl.BlockSpec((CHIP_ROWS, COLS), lambda i: (i, 0)),
            small,
            small,
            small,
            small,
        ],
        out_specs=pl.BlockSpec((1, 2 * TOK, LAST), lambda i: (i, 0, 0)),
        out_shape=pltpu.HBM((PEERS, 2 * TOK, LAST), bf16),
        compiler_params=params,
        name="pack",
    )(hidden, head, *[x.reshape(1, 128) for x in (targets, segments, mask, state)])


def spread_kernel(hidden, out, part, sems):
    start = pl.multiple_of((lax.axis_index("z") % 2) * STEP, STEP)
    copy = pltpu.make_async_copy(hidden.at[:, pl.ds(start, STEP)], part, sems.at[PEERS])
    copy.start()
    copy.wait()
    copies = [pltpu.make_async_copy(part, out.at[q], sems.at[q]) for q in range(PEERS)]
    for copy in copies:
        copy.start()
    for copy in copies:
        copy.wait()


def spread(hidden):
    return pl.pallas_call(
        spread_kernel,
        in_specs=[HBM],
        out_specs=ANY,
        out_shape=pltpu.HBM((PEERS, TOK, STEP), bf16),
        scratch_shapes=[
            pltpu.VMEM((TOK, STEP), bf16),
            pltpu.SemaphoreType.DMA((PEERS + 1,)),
        ],
        compiler_params=large,
        name="spread",
    )(hidden)


def gather_weight(source, q, rows, weight):
    for block in range(4):
        height = min(128, CHIP_ROWS - 128 * block)
        weight[128 * block : 128 * block + height, q * 128 : q * 128 + 128] = source[
            q, rows : rows + height, 128 * block : 128 * block + 128
        ]


def half_kernel(
    place, first, near, far, last, hidden, sent, partial, facts, weight, beside, rest, sems
):
    core = place[0]
    odd = place[2]
    rest_copies = [
        pltpu.make_async_copy(last.at[q], rest.at[q], sems.at[q]) for q in range(PEERS)
    ]
    beside_copies = [
        pltpu.make_async_copy(
            (near if q < 4 else far).at[q % 4], beside.at[q], sems.at[PEERS + q]
        )
        for q in range(PEERS)
    ]
    for q in range(PEERS):
        rest_copies[q].start()
        beside_copies[q].start()

    def fill(source, q, start, count):
        for i in range(count):
            column = start + i // 2 + 8 * (core if i % 2 == 0 else 1 - core)
            hidden[q * TOK : q * TOK + TOK, pl.ds(pl.multiple_of(column * 128, 128), 128)] = (
                source[q, :TOK, 128 * i : 128 * i + 128]
            )

    sent_copies = []
    for q in range(PEERS):
        fill(first, q, 3 * odd, 6)
        rest_copies[q].wait()
        fill(rest, q, 6, 4)
        gather_weight(rest, q, TOK, weight)
        beside_copies[q].wait()
        fill(beside, q, 3 - 3 * odd, 6)
        if q % 2 == 1:
            tokens = slice((q - 1) * TOK, (q + 1) * TOK)
            copy = pltpu.make_async_copy(
                hidden.at[tokens], sent.at[tokens], sems.at[2 * PEERS + q // 2]
            )
            copy.start()
            sent_copies.append(copy)
    facts[...] = rest[:, 2 * TOK - 16 :, LAST - 128 :]
    for block in range(4):
        tokens = slice(256 * block, 256 * block + 256)
        partial[:, tokens] = lax.dot_general(
            weight[...],
            hidden[tokens, : D // 2],
            (((1,), (1,)), ((), ())),
            preferred_element_type=f32,
        )
    for copy in sent_copies:
        copy.wait()


def half_call(place, first, near, far, last):
    return pl.pallas_call(
        half_kernel,
        in_specs=[SMEM, VMEM, ANY, ANY, ANY],
        out_specs=[VMEM, HBM, VMEM, VMEM],
        out_shape=[
            jax.ShapeDtypeStruct((TOKENS, D), bf16),
            pltpu.HBM((TOKENS, D), bf16),
            jax.ShapeDtypeStruct((CHIP_ROWS, TOKENS), f32),
            jax.ShapeDtypeStruct((PEERS, 16, 128), bf16),
        ],
        scratch_shapes=[
            pltpu.VMEM((CHIP_ROWS, D // 2), bf16),
            pltpu.VMEM((PEERS, TOK, STEP), bf16),
            pltpu.VMEM((PEERS, 2 * TOK, LAST), bf16),
            pltpu.SemaphoreType.DMA((2 * PEERS + 4,)),
        ],
        compiler_params=params,
        cost_estimate=pl.CostEstimate(
            flops=10**11, bytes_accessed=10**8, transcendentals=0
        ),
        name="half",
    )(place, first, near, far, last)


def logits_kernel(hidden, partial, other, logits, stats, facts, weight, table):
    facts[...] = other[:, 2 * TOK - 16 :, LAST - 128 :]
    for q in range(PEERS):
        gather_weight(other, q, TOK, weight)
    logits[CHIP_ROWS:, :] = jnp.zeros((8, TOKENS), f32)
    for block in range(4):
        tokens = slice(256 * block, 256 * block + 256)
        scores = partial[:, tokens] + lax.dot_general(
            weight[...],
            hidden[tokens, D // 2 :],
            (((1,), (1,)), ((), ())),
            preferred_element_type=f32,
        )
        logits[:CHIP_ROWS, tokens] = scores
        for half in range(2):
            part = scores[:, half * 128 : half * 128 + 128]
            q = block * 2 + half
            top = jnp.max(part, axis=0, keepdims=True)
            shifted = jnp.exp(part - top)
            exp_sum = jnp.sum(shifted, axis=0, keepdims=True)
            exp_dot = jnp.sum(shifted * part, axis=0, keepdims=True)
            table[q : q + 1, :] = top + jnp.log(exp_sum)
            table[8 + q : 9 + q, :] = exp_dot / exp_sum
    stats[...] = jnp.broadcast_to(table[...][None], (16, 16, 128))


def logits_call(hidden, partial, other):
    return pl.pallas_call(
        logits_kernel,
        in_specs=[VMEM] * 3,
        out_specs=[VMEM] * 3,
        out_shape=[
            jax.ShapeDtypeStruct((CHIP_ROWS + 8, TOKENS), f32),
            jax.ShapeDtypeStruct((16, 16, 128), f32),
            jax.ShapeDtypeStruct((PEERS, 16, 128), bf16),
        ],
        scratch_shapes=[
            pltpu.VMEM((CHIP_ROWS, D // 2), bf16),
            pltpu.VMEM((16, 128), f32),
        ],
        compiler_params=params,
        name="logits",
    )(hidden, partial, other)


def tokens_kernel(place, own_facts, other_facts, logits, tokens, state, facts):
    core = place[0]
    for q in range(PEERS):
        facts[2 * q + core] = own_facts[q].astype(f32)
        facts[2 * q + 1 - core] = other_facts[q].astype(f32)
    seg = lax.broadcasted_iota(jnp.int32, (SEGS, 128), 0).astype(f32)
    total = jnp.zeros((SEGS, 128), f32)
    for j in range(2 * PEERS):
        total = total + jnp.where(facts[j, 3:4, :] == seg, facts[j, 4:5, :], 0.0)
        state[j : j + 1, :] = facts[j, 5:6, :] + facts[j, 6:7, :] + facts[j, 7:8, :]
    counts = jnp.broadcast_to(jnp.sum(total, axis=1, keepdims=True), (SEGS, 128))
    row = lax.broadcasted_iota(jnp.int32, (CHIP_ROWS, 128), 0) + place[1]
    tokens[...] = jnp.zeros_like(tokens)
    for q in range(PEERS):
        lanes = slice(q * 128, q * 128 + 128)
        fact = facts[2 * q + core]
        goal = fact[0:1] * 65536.0 + fact[1:2] * 256.0 + fact[2:3]
        hit = row == goal.astype(jnp.int32)
        target_logit = jnp.sum(
            jnp.where(hit, logits[:CHIP_ROWS, lanes], 0.0), axis=0, keepdims=True
        )
        own_count = jnp.sum(jnp.where(fact[3:4] == seg, counts, 0.0), axis=0, keepdims=True)
        tok_weight = fact[4:5] / jnp.maximum(own_count, 1.0) / SEGS
        tokens[0:1, lanes] = tok_weight
        tokens[1:2, lanes] = goal
        tokens[2:3, lanes] = tok_weight * target_logit


def tokens_call(place, own_facts, other_facts, logits):
    return pl.pallas_call(
        tokens_kernel,
        in_specs=[SMEM] + [VMEM] * 3,
        out_specs=[VMEM] * 2,
        out_shape=[
            jax.ShapeDtypeStruct((8, TOKENS), f32),
            jax.ShapeDtypeStruct((16, 128), f32),
        ],
        scratch_shapes=[pltpu.VMEM((16, 16, 128), f32)],
        compiler_params=params,
        cost_estimate=pl.CostEstimate(
            flops=10**10, bytes_accessed=10**7, transcendentals=0
        ),
        name="tokens",
    )(place, own_facts, other_facts, logits)


def merged(stats):
    part, mean = stats[:, :8, :], stats[:, 8:, :]
    top = jnp.max(part, axis=0)
    share = jnp.exp(part - top[None])
    total = jnp.sum(share, axis=0)
    return top + jnp.log(total), jnp.sum(share * mean, axis=0) / total


def merge_kernel(stats, out):
    log_total, mean = merged(stats[...])
    out[:, :8, :] = jnp.broadcast_to(log_total[None], (16, 8, 128))
    out[:, 8:, :] = jnp.broadcast_to(mean[None], (16, 8, 128))


def merge_call(stats):
    return pl.pallas_call(
        merge_kernel,
        in_specs=[VMEM],
        out_specs=VMEM,
        out_shape=jax.ShapeDtypeStruct((16, 16, 128), f32),
        compiler_params=params,
        name="merge",
    )(stats)


def score_block(logits, tokens, log_total, entropy, base, row_start, q):
    lanes = slice(q * 128, q * 128 + 128)
    part = logits[pl.ds(pl.multiple_of(base, 8), PAD), lanes]
    row = lax.broadcasted_iota(jnp.int32, (PAD, 128), 0)
    tok_weight = tokens[0:1, lanes]
    goal = tokens[1:2, lanes].astype(jnp.int32)
    hit = (row + (row_start + base) == goal).astype(f32)
    above = part - log_total[q : q + 1, :]
    probability = jnp.exp(above)
    score = tok_weight * (
        probability - hit + penalty * probability * (above + entropy[q : q + 1, :])
    )
    return jnp.where(row < OWN, score, 0.0).astype(bf16)


def fetch(source, target, sems):
    copies = []
    for block in range(4):
        tokens = slice(block * 256, block * 256 + 256)
        copy = pltpu.make_async_copy(source.at[tokens], target.at[tokens], sems.at[block])
        copy.start()
        copies.append(copy)
    return copies


def away_kernel(place, stats, logits, tokens, hidden, score, totals, fetched, sems):
    copies = fetch(hidden, fetched, sems)
    core = place[0]
    log_total, mean = merged(stats[...])
    entropy = log_total - mean
    totals[:8, :] = log_total
    totals[8:, :] = entropy
    for q in range(PEERS):
        score[:, q * 128 : q * 128 + 128] = score_block(
            logits, tokens, log_total, entropy, (1 - core) * OWN, place[1], q
        )
    for copy in copies:
        copy.wait()


def away_call(place, stats, logits, tokens, hidden):
    return pl.pallas_call(
        away_kernel,
        in_specs=[SMEM, VMEM, VMEM, VMEM, HBM],
        out_specs=[VMEM] * 3,
        out_shape=[
            jax.ShapeDtypeStruct((PAD, TOKENS), bf16),
            jax.ShapeDtypeStruct((16, 128), f32),
            pltpu.VMEM((TOKENS, D), bf16),
        ],
        scratch_shapes=[pltpu.SemaphoreType.DMA((4,))],
        compiler_params=params,
        name="away",
    )(place, stats, logits, tokens, hidden)


def own_kernel(place, totals, logits, tokens, hidden, other, out, fetched, score, sems):
    copies = fetch(other, fetched, sems)
    for q in range(PEERS):
        score[:, q * 128 : q * 128 + 128] = score_block(
            logits, tokens, totals[:8, :], totals[8:, :], place[0] * OWN, place[1], q
        )
    for block in range(4):
        lanes = slice(block * 512, block * 512 + 512)
        out[:, lanes] = jnp.dot(score[...], hidden[:, lanes], preferred_element_type=f32)
    for copy in copies:
        copy.wait()


def own_call(place, totals, logits, tokens, hidden, other):
    return pl.pallas_call(
        own_kernel,
        in_specs=[SMEM] + [VMEM] * 4 + [HBM],
        out_specs=[VMEM] * 2,
        out_shape=[
            jax.ShapeDtypeStruct((PAD, D), f32),
            pltpu.VMEM((TOKENS, D), bf16),
        ],
        scratch_shapes=[
            pltpu.VMEM((PAD, TOKENS), bf16),
            pltpu.SemaphoreType.DMA((4,)),
        ],
        compiler_params=params,
        name="own",
    )(place, totals, logits, tokens, hidden, other)


def split_rows(value):
    high = value.astype(bf16).astype(f32)
    rest = value - high
    middle = rest.astype(bf16).astype(f32)
    return [high, middle, rest - middle]


def join_rows(total, start):
    return total[start : start + 1] + total[start + 1 : start + 2] + total[start + 2 : start + 3]


def grad_kernel(
    place, partial, score, hidden, state, totals, tokens, scaled, sums, grad, table
):
    core = place[0]
    places = [2 * i + core for i in range(8)] + [2 * i + 1 - core for i in range(8)]
    squares = jnp.zeros((PAD, 128), f32)
    for source in range(4):
        block = (source + 2) % 4
        lanes = slice(block * 512, block * 512 + 512)
        start = source * 512
        value = partial[:, lanes] + jnp.dot(
            score[...], hidden[:, start : start + 512], preferred_element_type=f32
        )
        grad[:, lanes] = value
        for i in range(4):
            part = value[:, 128 * i : 128 * i + 128]
            part = part * part
            squares = squares + part
            table[pl.ds(places[4 * block + i], 1), :] = jnp.sum(part, axis=0, keepdims=True)
    diagonal = lax.broadcasted_iota(jnp.int32, (PAD, PAD), 0) == lax.broadcasted_iota(
        jnp.int32, (PAD, PAD), 1
    )
    old = jnp.sum(jnp.where(diagonal, state[...], 0.0), axis=1, keepdims=True)
    row_new = decay_rate * old + (1.0 - decay_rate) * (
        jnp.sum(squares, axis=1, keepdims=True) / D
    )
    scale = jnp.broadcast_to(lax.rsqrt(row_new), (PAD, 128))
    row = lax.broadcasted_iota(jnp.int32, (PAD, 128), 0)
    lane = lax.broadcasted_iota(jnp.int32, (PAD, 128), 1)
    kept = jnp.where((row < OWN) & (lane == 0), jnp.broadcast_to(row_new, (PAD, 128)), 0.0)
    row_total = jnp.sum(kept, axis=0, keepdims=True)
    loss = jnp.zeros((1, 128), f32)
    for q in range(PEERS):
        lanes = slice(128 * q, 128 * q + 128)
        loss = loss + (
            tokens[0:1, lanes]
            * (totals[q : q + 1, :] - penalty * totals[8 + q : 9 + q, :])
            * (1.0 / 256.0)
            - tokens[2:3, lanes]
        )
    table[32:SUMS, :] = jnp.zeros((SUMS - 32, 128), f32)
    for i, line in enumerate(split_rows(row_total) + split_rows(loss)):
        table[32 + i : 33 + i, :] = line
    for i, j in enumerate(places):
        part = grad[:, 128 * i : 128 * i + 128] * scale
        scaled[:, pl.ds(pl.multiple_of(j * 128, 128), 128)] = part
        table[pl.ds(16 + j, 1), :] = jnp.sum(part * part, axis=0, keepdims=True)
    sums[...] = jnp.broadcast_to(table[...].astype(bf16)[None], (32, SUMS, 128))


def grad_call(place, partial, score, hidden, state, totals, tokens):
    return pl.pallas_call(
        grad_kernel,
        in_specs=[SMEM] + [VMEM] * 6,
        out_specs=[VMEM] * 2,
        out_shape=[
            jax.ShapeDtypeStruct((PAD, D), f32),
            jax.ShapeDtypeStruct((32, SUMS, 128), bf16),
        ],
        scratch_shapes=[
            pltpu.VMEM((PAD, D), f32),
            pltpu.VMEM((SUMS, 128), f32),
        ],
        compiler_params=params,
        name="grad",
    )(place, partial, score, hidden, state, totals, tokens)


def add_kernel(sums, out):
    total = jnp.sum(sums[...].astype(f32), axis=0)
    lines = split_rows(join_rows(total, 32)) + split_rows(join_rows(total, 35))
    row = lax.broadcasted_iota(jnp.int32, (SUMS, 128), 0)
    for i, line in enumerate(lines):
        total = jnp.where(row == 32 + i, line, total)
    out[...] = jnp.broadcast_to(total.astype(bf16)[None], (16, SUMS, 128))


def add_call(sums):
    return pl.pallas_call(
        add_kernel,
        in_specs=[VMEM],
        out_specs=VMEM,
        out_shape=jax.ShapeDtypeStruct((16, SUMS, 128), bf16),
        compiler_params=params,
        name="add",
    )(sums)


def update_kernel(sums, state, scaled, out, loss):
    total = jnp.sum(sums[...].astype(f32), axis=0)
    column_new = decay_rate * state[...] + (1.0 - decay_rate) * (total[:16] / V)
    column_scale = lax.rsqrt(column_new)
    row_mean = jnp.broadcast_to(jnp.sum(join_rows(total, 32), keepdims=True) / V, (16, 128))
    square_total = jnp.sum(total[16:32] * column_scale * column_scale, keepdims=True)
    square_total = row_mean * jnp.broadcast_to(square_total, (16, 128))
    update_rms = jnp.sqrt(square_total / (V * D))
    factor = jnp.sqrt(row_mean) * column_scale / jnp.maximum(1.0, update_rms / clip_limit)
    for j in range(16):
        out[j] = (scaled[:OWN, 128 * j : 128 * j + 128] * factor[j : j + 1, :]).astype(bf16)
    loss[...] = jnp.broadcast_to(jnp.sum(join_rows(total, 35), keepdims=True), (8, 128))


def update_call(sums, state, scaled):
    return pl.pallas_call(
        update_kernel,
        in_specs=[VMEM] * 3,
        out_specs=[VMEM] * 2,
        out_shape=[
            jax.ShapeDtypeStruct((16, OWN, 128), bf16),
            jax.ShapeDtypeStruct((8, 128), f32),
        ],
        compiler_params=params,
        name="update",
    )(sums, state, scaled)


def per_device(hidden, head_weight, targets, segments, loss_mask, row_state, column_state):
    core = lax.axis_index("core")
    chip = lax.axis_index(CHIPS)
    odd = lax.axis_index("z") % 2
    chip_start = chip * CHIP_ROWS
    place = jnp.stack([core, lax.axis_index(MP) * VOC + chip_start, odd]).astype(jnp.int32)
    own_state = lax.dynamic_slice_in_dim(row_state, chip_start + core * OWN, OWN, axis=0)
    own_state = jnp.concatenate([own_state, jnp.ones((PAD - OWN,), f32)]).reshape(1, PAD)
    place, own_state, targets = lax.optimization_barrier((place, own_state, targets))

    groups = [[4 * y + 2 * xh + (xh ^ k) for y in range(4) for xh in range(2)] for k in range(2)]
    first = lax.all_to_all(spread(hidden), PLANE, 0, 0, axis_index_groups=groups)
    last = pack(hidden, head_weight, targets, segments, loss_mask, column_state)
    last, first = lax.optimization_barrier((last, first))
    last = trade(last, CHIPS)
    near = lax.ppermute(first[:4], "z", [(i, i ^ 1) for i in range(16)])
    far = lax.ppermute(first[4:], "z", [(i, (i + 1 if i % 2 else i - 1) % 16) for i in range(16)])
    last_other = swap_cores(last)
    hidden_own, hidden_sent, partial, own_facts = half_call(place, first, near, far, last)
    logits, stats, other_facts = logits_call(hidden_own, partial, last_other)
    stats, hidden_sent = lax.optimization_barrier((stats, hidden_sent))
    tokens, state = tokens_call(place, own_facts, other_facts, logits)
    hidden_other = swap_cores(hidden_sent)
    stats = merge_call(trade(stats, PLANE))
    stats = trade(stats, "z")
    score_away, totals, hidden_own = away_call(place, stats, logits, tokens, hidden_sent)
    score_other = swap_cores(score_away)
    partial, hidden_other = own_call(
        place, totals, logits, tokens, hidden_own, hidden_other
    )
    scaled, sums = grad_call(
        place, partial, score_other, hidden_other, own_state, totals, tokens
    )
    sums = add_call(trade(sums, ("y", "xh", "core", "xl")))
    update, loss = update_call(trade(sums, "z"), state, scaled)
    update_step = trade(update, DP).reshape(VOC, COLS)
    return (update_step, loss[0, 0])


def solution(mesh):
    fine = Mesh(mesh.devices.reshape(4, 2, 2, 16, 2), AXES)
    return jax.shard_map(
        per_device,
        mesh=fine,
        in_specs=(P(DP, None), P(MP, DP), P(DP), P(DP), P(DP), P(MP), P(DP)),
        out_specs=(P(MP, DP), P()),
        check_vma=False,
    )
```

```python
import jax
import jax.numpy as jnp
from jax import lax
from jax.experimental import pallas as pl
from jax.experimental.pallas import tpu as pltpu
from jax.sharding import Mesh, PartitionSpec as P

D = 2048
V = 126976

penalty = 0.25
decay_rate = 1.0 - 16.0 ** (-0.8)
clip_limit = 1.0

AXES = ("y", "xh", "core", "z", "xl")
DP = ("y", "xh", "core")
MP = ("z", "xl")
CHIPS = ("y", "xh")
PLANE = ("y", "xh", "xl")

PEERS = 8
TOK = 128
COLS = 128
VOC = 3968
CHIP_ROWS = 496
OWN = 248
PAD = 256
TOKENS = 1024
SEGS = 64
SUMS = 40
STEP = 6 * 128
LAST = 4 * 128
f32 = jnp.float32
bf16 = jnp.bfloat16

params = pltpu.CompilerParams(vmem_limit_bytes=16 * 1024 * 1024)
large = pltpu.CompilerParams(vmem_limit_bytes=63 * 1024 * 1024 + 512 * 1024)
VMEM = pl.BlockSpec(memory_space=pltpu.VMEM)
SMEM = pl.BlockSpec(memory_space=pltpu.SMEM)
ANY = pl.BlockSpec(memory_space=pl.ANY)
HBM = pl.BlockSpec(memory_space=pltpu.HBM)


def swap_cores(value):
    return lax.ppermute(value, "core", [(0, 1), (1, 0)])


def trade(value, axes):
    return lax.all_to_all(value, axes, 0, 0)


def pack_kernel(hidden, head, targets, segments, mask, state, out):
    out[0, :TOK, :] = hidden[...]
    for block in range(4):
        height = min(128, CHIP_ROWS - 128 * block)
        out[0, TOK : TOK + height, 128 * block : 128 * block + 128] = head[
            128 * block : 128 * block + height, :
        ]
    row = lax.broadcasted_iota(jnp.int32, (16, 128), 0)
    goal = targets[...]
    value = state[...]
    high = value.astype(bf16).astype(f32)
    rest = value - high
    middle = rest.astype(bf16).astype(f32)
    facts = jnp.zeros((16, 128), f32)
    for place, fact in enumerate(
        [
            (goal >> 16).astype(f32),
            ((goal >> 8) & 255).astype(f32),
            (goal & 255).astype(f32),
            segments[...].astype(f32),
            mask[...].astype(f32),
            high,
            middle,
            rest - middle,
        ]
    ):
        facts = jnp.where(row == place, fact, facts)
    out[0, 2 * TOK - 16 :, LAST - 128 :] = facts.astype(bf16)


def pack(hidden, head, targets, segments, mask, state):
    small = pl.BlockSpec((1, 128), lambda i: (0, 0))
    return pl.pallas_call(
        pack_kernel,
        grid=(PEERS,),
        in_specs=[
            pl.BlockSpec((TOK, LAST), lambda i: (0, 3)),
            pl.BlockSpec((CHIP_ROWS, COLS), lambda i: (i, 0)),
            small,
            small,
            small,
            small,
        ],
        out_specs=pl.BlockSpec((1, 2 * TOK, LAST), lambda i: (i, 0, 0)),
        out_shape=pltpu.HBM((PEERS, 2 * TOK, LAST), bf16),
        compiler_params=params,
        name="pack",
    )(hidden, head, *[x.reshape(1, 128) for x in (targets, segments, mask, state)])


def spread_kernel(hidden, out, part, sems):
    start = pl.multiple_of((lax.axis_index("z") % 2) * STEP, STEP)
    copy = pltpu.make_async_copy(hidden.at[:, pl.ds(start, STEP)], part, sems.at[PEERS])
    copy.start()
    copy.wait()
    copies = [pltpu.make_async_copy(part, out.at[q], sems.at[q]) for q in range(PEERS)]
    for copy in copies:
        copy.start()
    for copy in copies:
        copy.wait()


def spread(hidden):
    return pl.pallas_call(
        spread_kernel,
        in_specs=[HBM],
        out_specs=ANY,
        out_shape=pltpu.HBM((PEERS, TOK, STEP), bf16),
        scratch_shapes=[
            pltpu.VMEM((TOK, STEP), bf16),
            pltpu.SemaphoreType.DMA((PEERS + 1,)),
        ],
        compiler_params=large,
        name="spread",
    )(hidden)


def gather_weight(source, q, rows, weight):
    for block in range(4):
        height = min(128, CHIP_ROWS - 128 * block)
        weight[128 * block : 128 * block + height, q * 128 : q * 128 + 128] = source[
            q, rows : rows + height, 128 * block : 128 * block + 128
        ]


def half_kernel(
    place, first, near, far, last, hidden, sent, partial, facts, weight, beside, rest, sems
):
    core = place[0]
    odd = place[2]
    pairs = PEERS // 2
    rest_copies, beside_copies = [], []
    for i in range(pairs):
        two = slice(2 * i, 2 * i + 2)
        copy = pltpu.make_async_copy(last.at[two], rest.at[two], sems.at[i])
        copy.start()
        rest_copies.append(copy)
        source = (near if i < 2 else far).at[slice(2 * (i % 2), 2 * (i % 2) + 2)]
        copy = pltpu.make_async_copy(source, beside.at[two], sems.at[pairs + i])
        copy.start()
        beside_copies.append(copy)

    def fill(source, q, start, count):
        for i in range(count):
            column = start + i // 2 + 8 * (core if i % 2 == 0 else 1 - core)
            hidden[q * TOK : q * TOK + TOK, pl.ds(pl.multiple_of(column * 128, 128), 128)] = (
                source[q, :TOK, 128 * i : 128 * i + 128]
            )

    sent_copies = []
    for q in range(PEERS):
        fill(first, q, 3 * odd, 6)
        if q % 2 == 0:
            rest_copies[q // 2].wait()
        fill(rest, q, 6, 4)
        gather_weight(rest, q, TOK, weight)
        if q % 2 == 0:
            beside_copies[q // 2].wait()
        fill(beside, q, 3 - 3 * odd, 6)
        if q % 2 == 1:
            tokens = slice((q - 1) * TOK, (q + 1) * TOK)
            copy = pltpu.make_async_copy(
                hidden.at[tokens], sent.at[tokens], sems.at[PEERS + q // 2]
            )
            copy.start()
            sent_copies.append(copy)
    facts[...] = rest[:, 2 * TOK - 16 :, LAST - 128 :]
    for block in range(4):
        tokens = slice(256 * block, 256 * block + 256)
        partial[:, tokens] = lax.dot_general(
            weight[...],
            hidden[tokens, : D // 2],
            (((1,), (1,)), ((), ())),
            preferred_element_type=f32,
        )
    for copy in sent_copies:
        copy.wait()


def half_call(place, first, near, far, last):
    return pl.pallas_call(
        half_kernel,
        in_specs=[SMEM, VMEM, ANY, ANY, ANY],
        out_specs=[VMEM, HBM, VMEM, VMEM],
        out_shape=[
            jax.ShapeDtypeStruct((TOKENS, D), bf16),
            pltpu.HBM((TOKENS, D), bf16),
            jax.ShapeDtypeStruct((CHIP_ROWS, TOKENS), f32),
            jax.ShapeDtypeStruct((PEERS, 16, 128), bf16),
        ],
        scratch_shapes=[
            pltpu.VMEM((CHIP_ROWS, D // 2), bf16),
            pltpu.VMEM((PEERS, TOK, STEP), bf16),
            pltpu.VMEM((PEERS, 2 * TOK, LAST), bf16),
            pltpu.SemaphoreType.DMA((PEERS + 4,)),
        ],
        compiler_params=params,
        cost_estimate=pl.CostEstimate(
            flops=10**11, bytes_accessed=10**8, transcendentals=0
        ),
        name="half",
    )(place, first, near, far, last)


def logits_kernel(hidden, partial, other, logits, stats, facts, weight, table):
    facts[...] = other[:, 2 * TOK - 16 :, LAST - 128 :]
    for q in range(PEERS):
        gather_weight(other, q, TOK, weight)
    logits[CHIP_ROWS:, :] = jnp.zeros((8, TOKENS), f32)
    for block in range(4):
        tokens = slice(256 * block, 256 * block + 256)
        scores = partial[:, tokens] + lax.dot_general(
            weight[...],
            hidden[tokens, D // 2 :],
            (((1,), (1,)), ((), ())),
            preferred_element_type=f32,
        )
        logits[:CHIP_ROWS, tokens] = scores
        for half in range(2):
            part = scores[:, half * 128 : half * 128 + 128]
            q = block * 2 + half
            top = jnp.max(part, axis=0, keepdims=True)
            shifted = jnp.exp(part - top)
            exp_sum = jnp.sum(shifted, axis=0, keepdims=True)
            exp_dot = jnp.sum(shifted * part, axis=0, keepdims=True)
            table[q : q + 1, :] = top + jnp.log(exp_sum)
            table[8 + q : 9 + q, :] = exp_dot / exp_sum
    stats[...] = jnp.broadcast_to(table[...][None], (16, 16, 128))


def logits_call(hidden, partial, other):
    return pl.pallas_call(
        logits_kernel,
        in_specs=[VMEM] * 3,
        out_specs=[VMEM] * 3,
        out_shape=[
            jax.ShapeDtypeStruct((CHIP_ROWS + 8, TOKENS), f32),
            jax.ShapeDtypeStruct((16, 16, 128), f32),
            jax.ShapeDtypeStruct((PEERS, 16, 128), bf16),
        ],
        scratch_shapes=[
            pltpu.VMEM((CHIP_ROWS, D // 2), bf16),
            pltpu.VMEM((16, 128), f32),
        ],
        compiler_params=params,
        name="logits",
    )(hidden, partial, other)


def tokens_kernel(place, own_facts, other_facts, logits, tokens, state, facts):
    core = place[0]
    for q in range(PEERS):
        facts[2 * q + core] = own_facts[q].astype(f32)
        facts[2 * q + 1 - core] = other_facts[q].astype(f32)
    seg = lax.broadcasted_iota(jnp.int32, (SEGS, 128), 0).astype(f32)
    total = jnp.zeros((SEGS, 128), f32)
    for j in range(2 * PEERS):
        total = total + jnp.where(facts[j, 3:4, :] == seg, facts[j, 4:5, :], 0.0)
        state[j : j + 1, :] = facts[j, 5:6, :] + facts[j, 6:7, :] + facts[j, 7:8, :]
    counts = jnp.broadcast_to(jnp.sum(total, axis=1, keepdims=True), (SEGS, 128))
    row = lax.broadcasted_iota(jnp.int32, (CHIP_ROWS, 128), 0) + place[1]
    tokens[...] = jnp.zeros_like(tokens)
    for q in range(PEERS):
        lanes = slice(q * 128, q * 128 + 128)
        fact = facts[2 * q + core]
        goal = fact[0:1] * 65536.0 + fact[1:2] * 256.0 + fact[2:3]
        hit = row == goal.astype(jnp.int32)
        target_logit = jnp.sum(
            jnp.where(hit, logits[:CHIP_ROWS, lanes], 0.0), axis=0, keepdims=True
        )
        own_count = jnp.sum(jnp.where(fact[3:4] == seg, counts, 0.0), axis=0, keepdims=True)
        tok_weight = fact[4:5] / jnp.maximum(own_count, 1.0) / SEGS
        tokens[0:1, lanes] = tok_weight
        tokens[1:2, lanes] = goal
        tokens[2:3, lanes] = tok_weight * target_logit


def tokens_call(place, own_facts, other_facts, logits):
    return pl.pallas_call(
        tokens_kernel,
        in_specs=[SMEM] + [VMEM] * 3,
        out_specs=[VMEM] * 2,
        out_shape=[
            jax.ShapeDtypeStruct((8, TOKENS), f32),
            jax.ShapeDtypeStruct((16, 128), f32),
        ],
        scratch_shapes=[pltpu.VMEM((16, 16, 128), f32)],
        compiler_params=params,
        cost_estimate=pl.CostEstimate(
            flops=10**10, bytes_accessed=10**7, transcendentals=0
        ),
        name="tokens",
    )(place, own_facts, other_facts, logits)


def merged(stats):
    part, mean = stats[:, :8, :], stats[:, 8:, :]
    top = jnp.max(part, axis=0)
    share = jnp.exp(part - top[None])
    total = jnp.sum(share, axis=0)
    return top + jnp.log(total), jnp.sum(share * mean, axis=0) / total


def merge_kernel(stats, out):
    log_total, mean = merged(stats[...])
    out[:, :8, :] = jnp.broadcast_to(log_total[None], (16, 8, 128))
    out[:, 8:, :] = jnp.broadcast_to(mean[None], (16, 8, 128))


def merge_call(stats):
    return pl.pallas_call(
        merge_kernel,
        in_specs=[VMEM],
        out_specs=VMEM,
        out_shape=jax.ShapeDtypeStruct((16, 16, 128), f32),
        compiler_params=params,
        name="merge",
    )(stats)


def score_block(logits, tokens, log_total, entropy, base, row_start, q):
    lanes = slice(q * 128, q * 128 + 128)
    part = logits[pl.ds(pl.multiple_of(base, 8), PAD), lanes]
    row = lax.broadcasted_iota(jnp.int32, (PAD, 128), 0)
    tok_weight = tokens[0:1, lanes]
    goal = tokens[1:2, lanes].astype(jnp.int32)
    hit = (row + (row_start + base) == goal).astype(f32)
    above = part - log_total[q : q + 1, :]
    probability = jnp.exp(above)
    score = tok_weight * (
        probability - hit + penalty * probability * (above + entropy[q : q + 1, :])
    )
    return jnp.where(row < OWN, score, 0.0).astype(bf16)


def fetch(source, target, sems):
    copies = []
    for block in range(2):
        tokens = slice(block * 512, block * 512 + 512)
        copy = pltpu.make_async_copy(source.at[tokens], target.at[tokens], sems.at[block])
        copy.start()
        copies.append(copy)
    return copies


def away_kernel(place, stats, logits, tokens, hidden, score, totals, fetched, sems):
    copies = fetch(hidden, fetched, sems)
    core = place[0]
    log_total, mean = merged(stats[...])
    entropy = log_total - mean
    totals[:8, :] = log_total
    totals[8:, :] = entropy
    for q in range(PEERS):
        score[:, q * 128 : q * 128 + 128] = score_block(
            logits, tokens, log_total, entropy, (1 - core) * OWN, place[1], q
        )
    for copy in copies:
        copy.wait()


def away_call(place, stats, logits, tokens, hidden):
    return pl.pallas_call(
        away_kernel,
        in_specs=[SMEM, VMEM, VMEM, VMEM, HBM],
        out_specs=[VMEM] * 3,
        out_shape=[
            jax.ShapeDtypeStruct((PAD, TOKENS), bf16),
            jax.ShapeDtypeStruct((16, 128), f32),
            pltpu.VMEM((TOKENS, D), bf16),
        ],
        scratch_shapes=[pltpu.SemaphoreType.DMA((2,))],
        compiler_params=params,
        name="away",
    )(place, stats, logits, tokens, hidden)


def own_kernel(place, totals, logits, tokens, hidden, other, out, fetched, score, sems):
    copies = fetch(other, fetched, sems)
    for q in range(PEERS):
        score[:, q * 128 : q * 128 + 128] = score_block(
            logits, tokens, totals[:8, :], totals[8:, :], place[0] * OWN, place[1], q
        )
    for block in range(4):
        lanes = slice(block * 512, block * 512 + 512)
        out[:, lanes] = jnp.dot(score[...], hidden[:, lanes], preferred_element_type=f32)
    for copy in copies:
        copy.wait()


def own_call(place, totals, logits, tokens, hidden, other):
    return pl.pallas_call(
        own_kernel,
        in_specs=[SMEM] + [VMEM] * 4 + [HBM],
        out_specs=[VMEM] * 2,
        out_shape=[
            jax.ShapeDtypeStruct((PAD, D), f32),
            pltpu.VMEM((TOKENS, D), bf16),
        ],
        scratch_shapes=[
            pltpu.VMEM((PAD, TOKENS), bf16),
            pltpu.SemaphoreType.DMA((2,)),
        ],
        compiler_params=params,
        name="own",
    )(place, totals, logits, tokens, hidden, other)


def split_rows(value):
    high = value.astype(bf16).astype(f32)
    rest = value - high
    middle = rest.astype(bf16).astype(f32)
    return [high, middle, rest - middle]


def join_rows(total, start):
    return total[start : start + 1] + total[start + 1 : start + 2] + total[start + 2 : start + 3]


def grad_kernel(
    place, partial, score, hidden, state, totals, tokens, scaled, sums, grad, table
):
    core = place[0]
    places = [2 * i + core for i in range(8)] + [2 * i + 1 - core for i in range(8)]
    squares = jnp.zeros((PAD, 128), f32)
    for source in range(4):
        block = (source + 2) % 4
        lanes = slice(block * 512, block * 512 + 512)
        start = source * 512
        value = partial[:, lanes] + jnp.dot(
            score[...], hidden[:, start : start + 512], preferred_element_type=f32
        )
        grad[:, lanes] = value
        for i in range(4):
            part = value[:, 128 * i : 128 * i + 128]
            part = part * part
            squares = squares + part
            table[pl.ds(places[4 * block + i], 1), :] = jnp.sum(part, axis=0, keepdims=True)
    diagonal = lax.broadcasted_iota(jnp.int32, (PAD, PAD), 0) == lax.broadcasted_iota(
        jnp.int32, (PAD, PAD), 1
    )
    old = jnp.sum(jnp.where(diagonal, state[...], 0.0), axis=1, keepdims=True)
    row_new = decay_rate * old + (1.0 - decay_rate) * (
        jnp.sum(squares, axis=1, keepdims=True) / D
    )
    scale = jnp.broadcast_to(lax.rsqrt(row_new), (PAD, 128))
    row = lax.broadcasted_iota(jnp.int32, (PAD, 128), 0)
    lane = lax.broadcasted_iota(jnp.int32, (PAD, 128), 1)
    kept = jnp.where((row < OWN) & (lane == 0), jnp.broadcast_to(row_new, (PAD, 128)), 0.0)
    row_total = jnp.sum(kept, axis=0, keepdims=True)
    loss = jnp.zeros((1, 128), f32)
    for q in range(PEERS):
        lanes = slice(128 * q, 128 * q + 128)
        loss = loss + (
            tokens[0:1, lanes]
            * (totals[q : q + 1, :] - penalty * totals[8 + q : 9 + q, :])
            * (1.0 / 256.0)
            - tokens[2:3, lanes]
        )
    table[32:SUMS, :] = jnp.zeros((SUMS - 32, 128), f32)
    for i, line in enumerate(split_rows(row_total) + split_rows(loss)):
        table[32 + i : 33 + i, :] = line
    for i, j in enumerate(places):
        part = grad[:, 128 * i : 128 * i + 128] * scale
        scaled[:, pl.ds(pl.multiple_of(j * 128, 128), 128)] = part
        table[pl.ds(16 + j, 1), :] = jnp.sum(part * part, axis=0, keepdims=True)
    sums[...] = jnp.broadcast_to(table[...].astype(bf16)[None], (32, SUMS, 128))


def grad_call(place, partial, score, hidden, state, totals, tokens):
    return pl.pallas_call(
        grad_kernel,
        in_specs=[SMEM] + [VMEM] * 6,
        out_specs=[VMEM] * 2,
        out_shape=[
            jax.ShapeDtypeStruct((PAD, D), f32),
            jax.ShapeDtypeStruct((32, SUMS, 128), bf16),
        ],
        scratch_shapes=[
            pltpu.VMEM((PAD, D), f32),
            pltpu.VMEM((SUMS, 128), f32),
        ],
        compiler_params=params,
        name="grad",
    )(place, partial, score, hidden, state, totals, tokens)


def add_kernel(sums, out):
    total = jnp.sum(sums[...].astype(f32), axis=0)
    lines = split_rows(join_rows(total, 32)) + split_rows(join_rows(total, 35))
    row = lax.broadcasted_iota(jnp.int32, (SUMS, 128), 0)
    for i, line in enumerate(lines):
        total = jnp.where(row == 32 + i, line, total)
    out[...] = jnp.broadcast_to(total.astype(bf16)[None], (16, SUMS, 128))


def add_call(sums):
    return pl.pallas_call(
        add_kernel,
        in_specs=[VMEM],
        out_specs=VMEM,
        out_shape=jax.ShapeDtypeStruct((16, SUMS, 128), bf16),
        compiler_params=params,
        name="add",
    )(sums)


def update_kernel(sums, state, scaled, out, loss):
    total = jnp.sum(sums[...].astype(f32), axis=0)
    column_new = decay_rate * state[...] + (1.0 - decay_rate) * (total[:16] / V)
    column_scale = lax.rsqrt(column_new)
    row_mean = jnp.broadcast_to(jnp.sum(join_rows(total, 32), keepdims=True) / V, (16, 128))
    square_total = jnp.sum(total[16:32] * column_scale * column_scale, keepdims=True)
    square_total = row_mean * jnp.broadcast_to(square_total, (16, 128))
    update_rms = jnp.sqrt(square_total / (V * D))
    factor = jnp.sqrt(row_mean) * column_scale / jnp.maximum(1.0, update_rms / clip_limit)
    for j in range(16):
        out[j] = (scaled[:OWN, 128 * j : 128 * j + 128] * factor[j : j + 1, :]).astype(bf16)
    loss[...] = jnp.sum(join_rows(total, 35), keepdims=True)


def update_call(sums, state, scaled):
    return pl.pallas_call(
        update_kernel,
        in_specs=[VMEM] * 3,
        out_specs=[VMEM] * 2,
        out_shape=[
            jax.ShapeDtypeStruct((16, OWN, 128), bf16),
            jax.ShapeDtypeStruct((1, 1), f32),
        ],
        compiler_params=params,
        name="update",
    )(sums, state, scaled)


def per_device(hidden, head_weight, targets, segments, loss_mask, row_state, column_state):
    core = lax.axis_index("core")
    chip = lax.axis_index(CHIPS)
    odd = lax.axis_index("z") % 2
    chip_start = chip * CHIP_ROWS
    place = jnp.stack([core, lax.axis_index(MP) * VOC + chip_start, odd]).astype(jnp.int32)
    own_state = lax.dynamic_slice_in_dim(row_state, chip_start + core * OWN, OWN, axis=0)
    own_state = jnp.concatenate([own_state, jnp.ones((PAD - OWN,), f32)]).reshape(1, PAD)
    place, own_state, targets = lax.optimization_barrier((place, own_state, targets))

    groups = [[4 * y + 2 * xh + (xh ^ k) for y in range(4) for xh in range(2)] for k in range(2)]
    first = lax.all_to_all(spread(hidden), PLANE, 0, 0, axis_index_groups=groups)
    last = pack(hidden, head_weight, targets, segments, loss_mask, column_state)
    last, first = lax.optimization_barrier((last, first))
    last = trade(last, CHIPS)
    near = lax.ppermute(first[:4], "z", [(i, i ^ 1) for i in range(16)])
    far = lax.ppermute(first[4:], "z", [(i, (i + 1 if i % 2 else i - 1) % 16) for i in range(16)])
    last_other = swap_cores(last)
    hidden_own, hidden_sent, partial, own_facts = half_call(place, first, near, far, last)
    logits, stats, other_facts = logits_call(hidden_own, partial, last_other)
    stats, hidden_sent = lax.optimization_barrier((stats, hidden_sent))
    tokens, state = tokens_call(place, own_facts, other_facts, logits)
    hidden_other = swap_cores(hidden_sent)
    stats = merge_call(trade(stats, PLANE))
    stats = trade(stats, "z")
    score_away, totals, hidden_own = away_call(place, stats, logits, tokens, hidden_sent)
    score_other = swap_cores(score_away)
    partial, hidden_other = own_call(
        place, totals, logits, tokens, hidden_own, hidden_other
    )
    scaled, sums = grad_call(
        place, partial, score_other, hidden_other, own_state, totals, tokens
    )
    sums = add_call(trade(sums, ("y", "xh", "core", "xl")))
    update, loss = update_call(trade(sums, "z"), state, scaled)
    update_step = trade(update, DP).reshape(VOC, COLS)
    return (update_step, loss.reshape(()))


def solution(mesh):
    fine = Mesh(mesh.devices.reshape(4, 2, 2, 16, 2), AXES)
    return jax.shard_map(
        per_device,
        mesh=fine,
        in_specs=(P(DP, None), P(MP, DP), P(DP), P(DP), P(DP), P(MP), P(DP)),
        out_specs=(P(MP, DP), P()),
        check_vma=False,
    )
```

```python
import jax
import jax.numpy as jnp
from jax import lax
from jax.experimental import pallas as pl
from jax.experimental.pallas import tpu as pltpu
from jax.sharding import Mesh, PartitionSpec as P

D = 2048
V = 126976

penalty = 0.25
decay_rate = 1.0 - 16.0 ** (-0.8)
clip_limit = 1.0

AXES = ("y", "xh", "core", "z", "xl")
DP = ("y", "xh", "core")
MP = ("z", "xl")
CHIPS = ("y", "xh")
PLANE = ("y", "xh", "xl")

PEERS = 8
TOK = 128
COLS = 128
VOC = 3968
CHIP_ROWS = 496
OWN = 248
PAD = 256
TOKENS = 1024
SEGS = 64
SUMS = 40
STEP = 8 * 128
LAST = 4 * 128
f32 = jnp.float32
bf16 = jnp.bfloat16

params = pltpu.CompilerParams(vmem_limit_bytes=16 * 1024 * 1024)
large = pltpu.CompilerParams(vmem_limit_bytes=63 * 1024 * 1024 + 512 * 1024)
VMEM = pl.BlockSpec(memory_space=pltpu.VMEM)
SMEM = pl.BlockSpec(memory_space=pltpu.SMEM)
ANY = pl.BlockSpec(memory_space=pl.ANY)
HBM = pl.BlockSpec(memory_space=pltpu.HBM)


def swap_cores(value):
    return lax.ppermute(value, "core", [(0, 1), (1, 0)])


def trade(value, axes):
    return lax.all_to_all(value, axes, 0, 0)


def pack_kernel(head, targets, segments, mask, state, out):
    for block in range(4):
        height = min(128, CHIP_ROWS - 128 * block)
        out[0, :height, 128 * block : 128 * block + 128] = head[
            128 * block : 128 * block + height, :
        ]
    row = lax.broadcasted_iota(jnp.int32, (16, 128), 0)
    goal = targets[...]
    value = state[...]
    high = value.astype(bf16).astype(f32)
    rest = value - high
    middle = rest.astype(bf16).astype(f32)
    facts = jnp.zeros((16, 128), f32)
    for place, fact in enumerate(
        [
            (goal >> 16).astype(f32),
            ((goal >> 8) & 255).astype(f32),
            (goal & 255).astype(f32),
            segments[...].astype(f32),
            mask[...].astype(f32),
            high,
            middle,
            rest - middle,
        ]
    ):
        facts = jnp.where(row == place, fact, facts)
    out[0, TOK - 16 :, LAST - 128 :] = facts.astype(bf16)


def pack(head, targets, segments, mask, state):
    small = pl.BlockSpec((1, 128), lambda i: (0, 0))
    return pl.pallas_call(
        pack_kernel,
        grid=(PEERS,),
        in_specs=[
            pl.BlockSpec((CHIP_ROWS, COLS), lambda i: (i, 0)),
            small,
            small,
            small,
            small,
        ],
        out_specs=pl.BlockSpec((1, TOK, LAST), lambda i: (i, 0, 0)),
        out_shape=pltpu.HBM((PEERS, TOK, LAST), bf16),
        compiler_params=params,
        name="pack",
    )(head, *[x.reshape(1, 128) for x in (targets, segments, mask, state)])


def spread_kernel(hidden, out, part, sems):
    start = pl.multiple_of((lax.axis_index("z") % 2) * STEP, STEP)
    copy = pltpu.make_async_copy(hidden.at[:, pl.ds(start, STEP)], part, sems.at[PEERS])
    copy.start()
    copy.wait()
    copies = [pltpu.make_async_copy(part, out.at[q], sems.at[q]) for q in range(PEERS)]
    for copy in copies:
        copy.start()
    for copy in copies:
        copy.wait()


def spread(hidden):
    return pl.pallas_call(
        spread_kernel,
        in_specs=[HBM],
        out_specs=ANY,
        out_shape=pltpu.HBM((PEERS, TOK, STEP), bf16),
        scratch_shapes=[
            pltpu.VMEM((TOK, STEP), bf16),
            pltpu.SemaphoreType.DMA((PEERS + 1,)),
        ],
        compiler_params=large,
        name="spread",
    )(hidden)


def gather_weight(source, q, weight):
    for block in range(4):
        height = min(128, CHIP_ROWS - 128 * block)
        weight[128 * block : 128 * block + height, q * 128 : q * 128 + 128] = source[
            q, :height, 128 * block : 128 * block + 128
        ]


def half_kernel(
    place, first, near, far, last, hidden, sent, partial, facts, weight, beside, rest, sems
):
    core = place[0]
    odd = place[2]
    pairs = PEERS // 2
    rest_copies, beside_copies = [], []
    for i in range(pairs):
        two = slice(2 * i, 2 * i + 2)
        copy = pltpu.make_async_copy(last.at[two], rest.at[two], sems.at[i])
        copy.start()
        rest_copies.append(copy)
        source = (near if i < 2 else far).at[slice(2 * (i % 2), 2 * (i % 2) + 2)]
        copy = pltpu.make_async_copy(source, beside.at[two], sems.at[pairs + i])
        copy.start()
        beside_copies.append(copy)

    def fill(source, q, start, count):
        for i in range(count):
            column = start + i // 2 + 8 * (core if i % 2 == 0 else 1 - core)
            hidden[q * TOK : q * TOK + TOK, pl.ds(pl.multiple_of(column * 128, 128), 128)] = (
                source[q, :TOK, 128 * i : 128 * i + 128]
            )

    sent_copies = []
    for q in range(PEERS):
        fill(first, q, 4 * odd, 8)
        if q % 2 == 0:
            rest_copies[q // 2].wait()
        gather_weight(rest, q, weight)
        if q % 2 == 0:
            beside_copies[q // 2].wait()
        fill(beside, q, 4 - 4 * odd, 8)
        if q % 2 == 1:
            tokens = slice((q - 1) * TOK, (q + 1) * TOK)
            copy = pltpu.make_async_copy(
                hidden.at[tokens], sent.at[tokens], sems.at[PEERS + q // 2]
            )
            copy.start()
            sent_copies.append(copy)
    facts[...] = rest[:, TOK - 16 :, LAST - 128 :]
    for block in range(4):
        tokens = slice(256 * block, 256 * block + 256)
        partial[:, tokens] = lax.dot_general(
            weight[...],
            hidden[tokens, : D // 2],
            (((1,), (1,)), ((), ())),
            preferred_element_type=f32,
        )
    for copy in sent_copies:
        copy.wait()


def half_call(place, first, near, far, last):
    return pl.pallas_call(
        half_kernel,
        in_specs=[SMEM, VMEM, ANY, ANY, ANY],
        out_specs=[VMEM, HBM, VMEM, VMEM],
        out_shape=[
            jax.ShapeDtypeStruct((TOKENS, D), bf16),
            pltpu.HBM((TOKENS, D), bf16),
            jax.ShapeDtypeStruct((CHIP_ROWS, TOKENS), f32),
            jax.ShapeDtypeStruct((PEERS, 16, 128), bf16),
        ],
        scratch_shapes=[
            pltpu.VMEM((CHIP_ROWS, D // 2), bf16),
            pltpu.VMEM((PEERS, TOK, STEP), bf16),
            pltpu.VMEM((PEERS, TOK, LAST), bf16),
            pltpu.SemaphoreType.DMA((PEERS + 4,)),
        ],
        compiler_params=params,
        cost_estimate=pl.CostEstimate(
            flops=10**11, bytes_accessed=10**8, transcendentals=0
        ),
        name="half",
    )(place, first, near, far, last)


def logits_kernel(hidden, partial, other, logits, stats, facts, weight, table):
    facts[...] = other[:, TOK - 16 :, LAST - 128 :]
    for q in range(PEERS):
        gather_weight(other, q, weight)
    logits[CHIP_ROWS:, :] = jnp.zeros((8, TOKENS), f32)
    for block in range(4):
        tokens = slice(256 * block, 256 * block + 256)
        scores = partial[:, tokens] + lax.dot_general(
            weight[...],
            hidden[tokens, D // 2 :],
            (((1,), (1,)), ((), ())),
            preferred_element_type=f32,
        )
        logits[:CHIP_ROWS, tokens] = scores
        for half in range(2):
            part = scores[:, half * 128 : half * 128 + 128]
            q = block * 2 + half
            top = jnp.max(part, axis=0, keepdims=True)
            shifted = jnp.exp(part - top)
            exp_sum = jnp.sum(shifted, axis=0, keepdims=True)
            exp_dot = jnp.sum(shifted * part, axis=0, keepdims=True)
            table[q : q + 1, :] = top + jnp.log(exp_sum)
            table[8 + q : 9 + q, :] = exp_dot / exp_sum
    stats[...] = jnp.broadcast_to(table[...][None], (16, 16, 128))


def logits_call(hidden, partial, other):
    return pl.pallas_call(
        logits_kernel,
        in_specs=[VMEM] * 3,
        out_specs=[VMEM] * 3,
        out_shape=[
            jax.ShapeDtypeStruct((CHIP_ROWS + 8, TOKENS), f32),
            jax.ShapeDtypeStruct((16, 16, 128), f32),
            jax.ShapeDtypeStruct((PEERS, 16, 128), bf16),
        ],
        scratch_shapes=[
            pltpu.VMEM((CHIP_ROWS, D // 2), bf16),
            pltpu.VMEM((16, 128), f32),
        ],
        compiler_params=params,
        name="logits",
    )(hidden, partial, other)


def tokens_kernel(place, own_facts, other_facts, logits, tokens, state, facts):
    core = place[0]
    for q in range(PEERS):
        facts[2 * q + core] = own_facts[q].astype(f32)
        facts[2 * q + 1 - core] = other_facts[q].astype(f32)
    seg = lax.broadcasted_iota(jnp.int32, (SEGS, 128), 0).astype(f32)
    total = jnp.zeros((SEGS, 128), f32)
    for j in range(2 * PEERS):
        total = total + jnp.where(facts[j, 3:4, :] == seg, facts[j, 4:5, :], 0.0)
        state[j : j + 1, :] = facts[j, 5:6, :] + facts[j, 6:7, :] + facts[j, 7:8, :]
    counts = jnp.broadcast_to(jnp.sum(total, axis=1, keepdims=True), (SEGS, 128))
    row = lax.broadcasted_iota(jnp.int32, (CHIP_ROWS, 128), 0) + place[1]
    tokens[...] = jnp.zeros_like(tokens)
    for q in range(PEERS):
        lanes = slice(q * 128, q * 128 + 128)
        fact = facts[2 * q + core]
        goal = fact[0:1] * 65536.0 + fact[1:2] * 256.0 + fact[2:3]
        hit = row == goal.astype(jnp.int32)
        target_logit = jnp.sum(
            jnp.where(hit, logits[:CHIP_ROWS, lanes], 0.0), axis=0, keepdims=True
        )
        own_count = jnp.sum(jnp.where(fact[3:4] == seg, counts, 0.0), axis=0, keepdims=True)
        tok_weight = fact[4:5] / jnp.maximum(own_count, 1.0) / SEGS
        tokens[0:1, lanes] = tok_weight
        tokens[1:2, lanes] = goal
        tokens[2:3, lanes] = tok_weight * target_logit


def tokens_call(place, own_facts, other_facts, logits):
    return pl.pallas_call(
        tokens_kernel,
        in_specs=[SMEM] + [VMEM] * 3,
        out_specs=[VMEM] * 2,
        out_shape=[
            jax.ShapeDtypeStruct((8, TOKENS), f32),
            jax.ShapeDtypeStruct((16, 128), f32),
        ],
        scratch_shapes=[pltpu.VMEM((16, 16, 128), f32)],
        compiler_params=params,
        cost_estimate=pl.CostEstimate(
            flops=10**10, bytes_accessed=10**7, transcendentals=0
        ),
        name="tokens",
    )(place, own_facts, other_facts, logits)


def merged(stats):
    part, mean = stats[:, :8, :], stats[:, 8:, :]
    top = jnp.max(part, axis=0)
    share = jnp.exp(part - top[None])
    total = jnp.sum(share, axis=0)
    return top + jnp.log(total), jnp.sum(share * mean, axis=0) / total


def merge_kernel(stats, out):
    log_total, mean = merged(stats[...])
    out[:, :8, :] = jnp.broadcast_to(log_total[None], (16, 8, 128))
    out[:, 8:, :] = jnp.broadcast_to(mean[None], (16, 8, 128))


def merge_call(stats):
    return pl.pallas_call(
        merge_kernel,
        in_specs=[VMEM],
        out_specs=VMEM,
        out_shape=jax.ShapeDtypeStruct((16, 16, 128), f32),
        compiler_params=params,
        name="merge",
    )(stats)


def score_block(logits, tokens, log_total, entropy, base, row_start, q):
    lanes = slice(q * 128, q * 128 + 128)
    part = logits[pl.ds(pl.multiple_of(base, 8), PAD), lanes]
    row = lax.broadcasted_iota(jnp.int32, (PAD, 128), 0)
    tok_weight = tokens[0:1, lanes]
    goal = tokens[1:2, lanes].astype(jnp.int32)
    hit = (row + (row_start + base) == goal).astype(f32)
    above = part - log_total[q : q + 1, :]
    probability = jnp.exp(above)
    score = tok_weight * (
        probability - hit + penalty * probability * (above + entropy[q : q + 1, :])
    )
    return jnp.where(row < OWN, score, 0.0).astype(bf16)


def fetch(source, target, sems):
    copies = []
    for block in range(2):
        tokens = slice(block * 512, block * 512 + 512)
        copy = pltpu.make_async_copy(source.at[tokens], target.at[tokens], sems.at[block])
        copy.start()
        copies.append(copy)
    return copies


def away_kernel(place, stats, logits, tokens, hidden, score, totals, fetched, sems):
    copies = fetch(hidden, fetched, sems)
    core = place[0]
    log_total, mean = merged(stats[...])
    entropy = log_total - mean
    totals[:8, :] = log_total
    totals[8:, :] = entropy
    for q in range(PEERS):
        score[:, q * 128 : q * 128 + 128] = score_block(
            logits, tokens, log_total, entropy, (1 - core) * OWN, place[1], q
        )
    for copy in copies:
        copy.wait()


def away_call(place, stats, logits, tokens, hidden):
    return pl.pallas_call(
        away_kernel,
        in_specs=[SMEM, VMEM, VMEM, VMEM, HBM],
        out_specs=[VMEM] * 3,
        out_shape=[
            jax.ShapeDtypeStruct((PAD, TOKENS), bf16),
            jax.ShapeDtypeStruct((16, 128), f32),
            pltpu.VMEM((TOKENS, D), bf16),
        ],
        scratch_shapes=[pltpu.SemaphoreType.DMA((2,))],
        compiler_params=params,
        name="away",
    )(place, stats, logits, tokens, hidden)


def own_kernel(place, totals, logits, tokens, hidden, other, out, fetched, score, sems):
    copies = fetch(other, fetched, sems)
    for q in range(PEERS):
        score[:, q * 128 : q * 128 + 128] = score_block(
            logits, tokens, totals[:8, :], totals[8:, :], place[0] * OWN, place[1], q
        )
    for block in range(4):
        lanes = slice(block * 512, block * 512 + 512)
        out[:, lanes] = jnp.dot(score[...], hidden[:, lanes], preferred_element_type=f32)
    for copy in copies:
        copy.wait()


def own_call(place, totals, logits, tokens, hidden, other):
    return pl.pallas_call(
        own_kernel,
        in_specs=[SMEM] + [VMEM] * 4 + [HBM],
        out_specs=[VMEM] * 2,
        out_shape=[
            jax.ShapeDtypeStruct((PAD, D), f32),
            pltpu.VMEM((TOKENS, D), bf16),
        ],
        scratch_shapes=[
            pltpu.VMEM((PAD, TOKENS), bf16),
            pltpu.SemaphoreType.DMA((2,)),
        ],
        compiler_params=params,
        name="own",
    )(place, totals, logits, tokens, hidden, other)


def split_rows(value):
    high = value.astype(bf16).astype(f32)
    rest = value - high
    middle = rest.astype(bf16).astype(f32)
    return [high, middle, rest - middle]


def join_rows(total, start):
    return total[start : start + 1] + total[start + 1 : start + 2] + total[start + 2 : start + 3]


def grad_kernel(
    place, partial, score, hidden, state, totals, tokens, scaled, sums, grad, table
):
    core = place[0]
    places = [2 * i + core for i in range(8)] + [2 * i + 1 - core for i in range(8)]
    squares = jnp.zeros((PAD, 128), f32)
    for source in range(4):
        block = (source + 2) % 4
        lanes = slice(block * 512, block * 512 + 512)
        start = source * 512
        value = partial[:, lanes] + jnp.dot(
            score[...], hidden[:, start : start + 512], preferred_element_type=f32
        )
        grad[:, lanes] = value
        for i in range(4):
            part = value[:, 128 * i : 128 * i + 128]
            part = part * part
            squares = squares + part
            table[pl.ds(places[4 * block + i], 1), :] = jnp.sum(part, axis=0, keepdims=True)
    diagonal = lax.broadcasted_iota(jnp.int32, (PAD, PAD), 0) == lax.broadcasted_iota(
        jnp.int32, (PAD, PAD), 1
    )
    old = jnp.sum(jnp.where(diagonal, state[...], 0.0), axis=1, keepdims=True)
    row_new = decay_rate * old + (1.0 - decay_rate) * (
        jnp.sum(squares, axis=1, keepdims=True) / D
    )
    scale = jnp.broadcast_to(lax.rsqrt(row_new), (PAD, 128))
    row = lax.broadcasted_iota(jnp.int32, (PAD, 128), 0)
    lane = lax.broadcasted_iota(jnp.int32, (PAD, 128), 1)
    kept = jnp.where((row < OWN) & (lane == 0), jnp.broadcast_to(row_new, (PAD, 128)), 0.0)
    row_total = jnp.sum(kept, axis=0, keepdims=True)
    loss = jnp.zeros((1, 128), f32)
    for q in range(PEERS):
        lanes = slice(128 * q, 128 * q + 128)
        loss = loss + (
            tokens[0:1, lanes]
            * (totals[q : q + 1, :] - penalty * totals[8 + q : 9 + q, :])
            * (1.0 / 256.0)
            - tokens[2:3, lanes]
        )
    table[32:SUMS, :] = jnp.zeros((SUMS - 32, 128), f32)
    for i, line in enumerate(split_rows(row_total) + split_rows(loss)):
        table[32 + i : 33 + i, :] = line
    for i, j in enumerate(places):
        part = grad[:, 128 * i : 128 * i + 128] * scale
        scaled[:, pl.ds(pl.multiple_of(j * 128, 128), 128)] = part
        table[pl.ds(16 + j, 1), :] = jnp.sum(part * part, axis=0, keepdims=True)
    sums[...] = jnp.broadcast_to(table[...].astype(bf16)[None], (32, SUMS, 128))


def grad_call(place, partial, score, hidden, state, totals, tokens):
    return pl.pallas_call(
        grad_kernel,
        in_specs=[SMEM] + [VMEM] * 6,
        out_specs=[VMEM] * 2,
        out_shape=[
            jax.ShapeDtypeStruct((PAD, D), f32),
            jax.ShapeDtypeStruct((32, SUMS, 128), bf16),
        ],
        scratch_shapes=[
            pltpu.VMEM((PAD, D), f32),
            pltpu.VMEM((SUMS, 128), f32),
        ],
        compiler_params=params,
        name="grad",
    )(place, partial, score, hidden, state, totals, tokens)


def add_kernel(sums, out):
    total = jnp.sum(sums[...].astype(f32), axis=0)
    lines = split_rows(join_rows(total, 32)) + split_rows(join_rows(total, 35))
    row = lax.broadcasted_iota(jnp.int32, (SUMS, 128), 0)
    for i, line in enumerate(lines):
        total = jnp.where(row == 32 + i, line, total)
    out[...] = jnp.broadcast_to(total.astype(bf16)[None], (16, SUMS, 128))


def add_call(sums):
    return pl.pallas_call(
        add_kernel,
        in_specs=[VMEM],
        out_specs=VMEM,
        out_shape=jax.ShapeDtypeStruct((16, SUMS, 128), bf16),
        compiler_params=params,
        name="add",
    )(sums)


def update_kernel(sums, state, scaled, out, loss):
    total = jnp.sum(sums[...].astype(f32), axis=0)
    column_new = decay_rate * state[...] + (1.0 - decay_rate) * (total[:16] / V)
    column_scale = lax.rsqrt(column_new)
    row_mean = jnp.broadcast_to(jnp.sum(join_rows(total, 32), keepdims=True) / V, (16, 128))
    square_total = jnp.sum(total[16:32] * column_scale * column_scale, keepdims=True)
    square_total = row_mean * jnp.broadcast_to(square_total, (16, 128))
    update_rms = jnp.sqrt(square_total / (V * D))
    factor = jnp.sqrt(row_mean) * column_scale / jnp.maximum(1.0, update_rms / clip_limit)
    for j in range(16):
        out[j] = (scaled[:OWN, 128 * j : 128 * j + 128] * factor[j : j + 1, :]).astype(bf16)
    loss[...] = jnp.sum(join_rows(total, 35), keepdims=True)


def update_call(sums, state, scaled):
    return pl.pallas_call(
        update_kernel,
        in_specs=[VMEM] * 3,
        out_specs=[VMEM] * 2,
        out_shape=[
            jax.ShapeDtypeStruct((16, OWN, 128), bf16),
            jax.ShapeDtypeStruct((1, 1), f32),
        ],
        compiler_params=params,
        name="update",
    )(sums, state, scaled)


def per_device(hidden, head_weight, targets, segments, loss_mask, row_state, column_state):
    core = lax.axis_index("core")
    chip = lax.axis_index(CHIPS)
    odd = lax.axis_index("z") % 2
    chip_start = chip * CHIP_ROWS
    place = jnp.stack([core, lax.axis_index(MP) * VOC + chip_start, odd]).astype(jnp.int32)
    own_state = lax.dynamic_slice_in_dim(row_state, chip_start + core * OWN, OWN, axis=0)
    own_state = jnp.concatenate([own_state, jnp.ones((PAD - OWN,), f32)]).reshape(1, PAD)
    place, own_state, targets = lax.optimization_barrier((place, own_state, targets))

    groups = [[4 * y + 2 * xh + (xh ^ k) for y in range(4) for xh in range(2)] for k in range(2)]
    first = lax.all_to_all(spread(hidden), PLANE, 0, 0, axis_index_groups=groups)
    last = pack(head_weight, targets, segments, loss_mask, column_state)
    last, first = lax.optimization_barrier((last, first))
    last = trade(last, CHIPS)
    near = lax.ppermute(first[:4], "z", [(i, i ^ 1) for i in range(16)])
    far = lax.ppermute(first[4:], "z", [(i, (i + 1 if i % 2 else i - 1) % 16) for i in range(16)])
    last_other = swap_cores(last)
    hidden_own, hidden_sent, partial, own_facts = half_call(place, first, near, far, last)
    logits, stats, other_facts = logits_call(hidden_own, partial, last_other)
    stats, hidden_sent = lax.optimization_barrier((stats, hidden_sent))
    tokens, state = tokens_call(place, own_facts, other_facts, logits)
    hidden_other = swap_cores(hidden_sent)
    stats = merge_call(trade(stats, PLANE))
    stats = trade(stats, "z")
    score_away, totals, hidden_own = away_call(place, stats, logits, tokens, hidden_sent)
    score_other = swap_cores(score_away)
    partial, hidden_other = own_call(
        place, totals, logits, tokens, hidden_own, hidden_other
    )
    scaled, sums = grad_call(
        place, partial, score_other, hidden_other, own_state, totals, tokens
    )
    sums = add_call(trade(sums, ("y", "xh", "core", "xl")))
    update, loss = update_call(trade(sums, "z"), state, scaled)
    update_step = trade(update, DP).reshape(VOC, COLS)
    return (update_step, loss.reshape(()))


def solution(mesh):
    fine = Mesh(mesh.devices.reshape(4, 2, 2, 16, 2), AXES)
    return jax.shard_map(
        per_device,
        mesh=fine,
        in_specs=(P(DP, None), P(MP, DP), P(DP), P(DP), P(DP), P(MP), P(DP)),
        out_specs=(P(MP, DP), P()),
        check_vma=False,
    )
```

```python
import jax
import jax.numpy as jnp
from jax import lax
from jax.experimental import pallas as pl
from jax.experimental.pallas import tpu as pltpu
from jax.sharding import Mesh, PartitionSpec as P

D = 2048
V = 126976

penalty = 0.25
decay_rate = 1.0 - 16.0 ** (-0.8)
clip_limit = 1.0

AXES = ("y", "xh", "core", "z", "xl")
DP = ("y", "xh", "core")
MP = ("z", "xl")
CHIPS = ("y", "xh")
PLANE = ("y", "xh", "xl")

PEERS = 8
TOK = 128
COLS = 128
VOC = 3968
CHIP_ROWS = 496
OWN = 248
PAD = 256
TOKENS = 1024
SEGS = 64
SUMS = 40
STEP = 6 * 128
LAST = 4 * 128
f32 = jnp.float32
bf16 = jnp.bfloat16

params = pltpu.CompilerParams(vmem_limit_bytes=16 * 1024 * 1024)
large = pltpu.CompilerParams(vmem_limit_bytes=63 * 1024 * 1024 + 512 * 1024)
VMEM = pl.BlockSpec(memory_space=pltpu.VMEM)
SMEM = pl.BlockSpec(memory_space=pltpu.SMEM)
ANY = pl.BlockSpec(memory_space=pl.ANY)
HBM = pl.BlockSpec(memory_space=pltpu.HBM)


def swap_cores(value):
    return lax.ppermute(value, "core", [(0, 1), (1, 0)])


def trade(value, axes):
    return lax.all_to_all(value, axes, 0, 0)


def pack_kernel(hidden, head, targets, segments, mask, state, out):
    out[0, :TOK, :] = hidden[...]
    for block in range(4):
        height = min(128, CHIP_ROWS - 128 * block)
        out[0, TOK : TOK + height, 128 * block : 128 * block + 128] = head[
            128 * block : 128 * block + height, :
        ]
    row = lax.broadcasted_iota(jnp.int32, (16, 128), 0)
    goal = targets[...]
    value = state[...]
    high = value.astype(bf16).astype(f32)
    rest = value - high
    middle = rest.astype(bf16).astype(f32)
    facts = jnp.zeros((16, 128), f32)
    for place, fact in enumerate(
        [
            (goal >> 16).astype(f32),
            ((goal >> 8) & 255).astype(f32),
            (goal & 255).astype(f32),
            segments[...].astype(f32),
            mask[...].astype(f32),
            high,
            middle,
            rest - middle,
        ]
    ):
        facts = jnp.where(row == place, fact, facts)
    out[0, 2 * TOK - 16 :, LAST - 128 :] = facts.astype(bf16)


def pack(hidden, head, targets, segments, mask, state):
    small = pl.BlockSpec((1, 128), lambda i: (0, 0))
    return pl.pallas_call(
        pack_kernel,
        grid=(PEERS,),
        in_specs=[
            pl.BlockSpec((TOK, LAST), lambda i: (0, 3)),
            pl.BlockSpec((CHIP_ROWS, COLS), lambda i: (i, 0)),
            small,
            small,
            small,
            small,
        ],
        out_specs=pl.BlockSpec((1, 2 * TOK, LAST), lambda i: (i, 0, 0)),
        out_shape=pltpu.HBM((PEERS, 2 * TOK, LAST), bf16),
        compiler_params=params,
        name="pack",
    )(hidden, head, *[x.reshape(1, 128) for x in (targets, segments, mask, state)])


def spread_kernel(hidden, out, part, sems):
    start = pl.multiple_of((lax.axis_index("z") % 2) * STEP, STEP)
    copy = pltpu.make_async_copy(hidden.at[:, pl.ds(start, STEP)], part, sems.at[PEERS])
    copy.start()
    copy.wait()
    copies = [pltpu.make_async_copy(part, out.at[q], sems.at[q]) for q in range(PEERS)]
    for copy in copies:
        copy.start()
    for copy in copies:
        copy.wait()


def spread(hidden):
    return pl.pallas_call(
        spread_kernel,
        in_specs=[HBM],
        out_specs=ANY,
        out_shape=pltpu.HBM((PEERS, TOK, STEP), bf16),
        scratch_shapes=[
            pltpu.VMEM((TOK, STEP), bf16),
            pltpu.SemaphoreType.DMA((PEERS + 1,)),
        ],
        compiler_params=large,
        name="spread",
    )(hidden)


def gather_weight(source, q, rows, weight):
    for block in range(4):
        height = min(128, CHIP_ROWS - 128 * block)
        weight[128 * block : 128 * block + height, q * 128 : q * 128 + 128] = source[
            q, rows : rows + height, 128 * block : 128 * block + 128
        ]


def half_kernel(
    place, first, near, far, last, hidden, sent, partial, facts, weight, beside, rest, sems
):
    core = place[0]
    odd = place[2]
    pairs = PEERS // 2
    rest_copies, beside_copies = [], {}
    for i in range(pairs):
        two = slice(2 * i, 2 * i + 2)
        copy = pltpu.make_async_copy(last.at[two], rest.at[two], sems.at[i])
        copy.start()
        rest_copies.append(copy)

    cuts = [(near, 0, 2, 0), (near, 2, 4, 2), (near, 4, 5, 4), (far, 0, 1, 5), (far, 1, 3, 6)]
    for i, (source, low, high, q) in enumerate(cuts):
        copy = pltpu.make_async_copy(
            source.at[low:high], beside.at[q : q + high - low], sems.at[PEERS + i]
        )
        copy.start()
        beside_copies[q] = copy

    def fill(source, q, start, count):
        for i in range(count):
            column = start + i // 2 + 8 * (core if i % 2 == 0 else 1 - core)
            hidden[q * TOK : q * TOK + TOK, pl.ds(pl.multiple_of(column * 128, 128), 128)] = (
                source[q, :TOK, 128 * i : 128 * i + 128]
            )

    sent_copies = []
    for q in range(PEERS):
        fill(first, q, 3 * odd, 6)
        if q % 2 == 0:
            rest_copies[q // 2].wait()
        fill(rest, q, 6, 4)
        gather_weight(rest, q, TOK, weight)
        if q in beside_copies:
            beside_copies[q].wait()
        fill(beside, q, 3 - 3 * odd, 6)
        if q % 2 == 1:
            tokens = slice((q - 1) * TOK, (q + 1) * TOK)
            copy = pltpu.make_async_copy(
                hidden.at[tokens], sent.at[tokens], sems.at[4 + q // 2]
            )
            copy.start()
            sent_copies.append(copy)
    facts[...] = rest[:, 2 * TOK - 16 :, LAST - 128 :]
    for block in range(4):
        tokens = slice(256 * block, 256 * block + 256)
        partial[:, tokens] = lax.dot_general(
            weight[...],
            hidden[tokens, : D // 2],
            (((1,), (1,)), ((), ())),
            preferred_element_type=f32,
        )
    for copy in sent_copies:
        copy.wait()


def half_call(place, first, near, far, last):
    return pl.pallas_call(
        half_kernel,
        in_specs=[SMEM, VMEM, ANY, ANY, ANY],
        out_specs=[VMEM, HBM, VMEM, VMEM],
        out_shape=[
            jax.ShapeDtypeStruct((TOKENS, D), bf16),
            pltpu.HBM((TOKENS, D), bf16),
            jax.ShapeDtypeStruct((CHIP_ROWS, TOKENS), f32),
            jax.ShapeDtypeStruct((PEERS, 16, 128), bf16),
        ],
        scratch_shapes=[
            pltpu.VMEM((CHIP_ROWS, D // 2), bf16),
            pltpu.VMEM((PEERS, TOK, STEP), bf16),
            pltpu.VMEM((PEERS, 2 * TOK, LAST), bf16),
            pltpu.SemaphoreType.DMA((PEERS + 5,)),
        ],
        compiler_params=params,
        cost_estimate=pl.CostEstimate(
            flops=10**11, bytes_accessed=10**8, transcendentals=0
        ),
        name="half",
    )(place, first, near, far, last)


def logits_kernel(hidden, partial, other, logits, stats, facts, weight, table):
    facts[...] = other[:, 2 * TOK - 16 :, LAST - 128 :]
    for q in range(PEERS):
        gather_weight(other, q, TOK, weight)
    logits[CHIP_ROWS:, :] = jnp.zeros((8, TOKENS), f32)
    for block in range(4):
        tokens = slice(256 * block, 256 * block + 256)
        scores = partial[:, tokens] + lax.dot_general(
            weight[...],
            hidden[tokens, D // 2 :],
            (((1,), (1,)), ((), ())),
            preferred_element_type=f32,
        )
        logits[:CHIP_ROWS, tokens] = scores
        for half in range(2):
            part = scores[:, half * 128 : half * 128 + 128]
            q = block * 2 + half
            top = jnp.max(part, axis=0, keepdims=True)
            shifted = jnp.exp(part - top)
            exp_sum = jnp.sum(shifted, axis=0, keepdims=True)
            exp_dot = jnp.sum(shifted * part, axis=0, keepdims=True)
            table[q : q + 1, :] = top + jnp.log(exp_sum)
            table[8 + q : 9 + q, :] = exp_dot / exp_sum
    stats[...] = jnp.broadcast_to(table[...][None], (16, 16, 128))


def logits_call(hidden, partial, other):
    return pl.pallas_call(
        logits_kernel,
        in_specs=[VMEM] * 3,
        out_specs=[VMEM] * 3,
        out_shape=[
            jax.ShapeDtypeStruct((CHIP_ROWS + 8, TOKENS), f32),
            jax.ShapeDtypeStruct((16, 16, 128), f32),
            jax.ShapeDtypeStruct((PEERS, 16, 128), bf16),
        ],
        scratch_shapes=[
            pltpu.VMEM((CHIP_ROWS, D // 2), bf16),
            pltpu.VMEM((16, 128), f32),
        ],
        compiler_params=params,
        name="logits",
    )(hidden, partial, other)


def tokens_kernel(place, own_facts, other_facts, logits, tokens, state, facts):
    core = place[0]
    for q in range(PEERS):
        facts[2 * q + core] = own_facts[q].astype(f32)
        facts[2 * q + 1 - core] = other_facts[q].astype(f32)
    seg = lax.broadcasted_iota(jnp.int32, (SEGS, 128), 0).astype(f32)
    total = jnp.zeros((SEGS, 128), f32)
    for j in range(2 * PEERS):
        total = total + jnp.where(facts[j, 3:4, :] == seg, facts[j, 4:5, :], 0.0)
        state[j : j + 1, :] = facts[j, 5:6, :] + facts[j, 6:7, :] + facts[j, 7:8, :]
    counts = jnp.broadcast_to(jnp.sum(total, axis=1, keepdims=True), (SEGS, 128))
    row = lax.broadcasted_iota(jnp.int32, (CHIP_ROWS, 128), 0) + place[1]
    tokens[...] = jnp.zeros_like(tokens)
    for q in range(PEERS):
        lanes = slice(q * 128, q * 128 + 128)
        fact = facts[2 * q + core]
        goal = fact[0:1] * 65536.0 + fact[1:2] * 256.0 + fact[2:3]
        hit = row == goal.astype(jnp.int32)
        target_logit = jnp.sum(
            jnp.where(hit, logits[:CHIP_ROWS, lanes], 0.0), axis=0, keepdims=True
        )
        own_count = jnp.sum(jnp.where(fact[3:4] == seg, counts, 0.0), axis=0, keepdims=True)
        tok_weight = fact[4:5] / jnp.maximum(own_count, 1.0) / SEGS
        tokens[0:1, lanes] = tok_weight
        tokens[1:2, lanes] = goal
        tokens[2:3, lanes] = tok_weight * target_logit


def tokens_call(place, own_facts, other_facts, logits):
    return pl.pallas_call(
        tokens_kernel,
        in_specs=[SMEM] + [VMEM] * 3,
        out_specs=[VMEM] * 2,
        out_shape=[
            jax.ShapeDtypeStruct((8, TOKENS), f32),
            jax.ShapeDtypeStruct((16, 128), f32),
        ],
        scratch_shapes=[pltpu.VMEM((16, 16, 128), f32)],
        compiler_params=params,
        cost_estimate=pl.CostEstimate(
            flops=10**10, bytes_accessed=10**7, transcendentals=0
        ),
        name="tokens",
    )(place, own_facts, other_facts, logits)


def merged(stats):
    part, mean = stats[:, :8, :], stats[:, 8:, :]
    top = jnp.max(part, axis=0)
    share = jnp.exp(part - top[None])
    total = jnp.sum(share, axis=0)
    return top + jnp.log(total), jnp.sum(share * mean, axis=0) / total


def merge_kernel(stats, out):
    log_total, mean = merged(stats[...])
    out[:, :8, :] = jnp.broadcast_to(log_total[None], (16, 8, 128))
    out[:, 8:, :] = jnp.broadcast_to(mean[None], (16, 8, 128))


def merge_call(stats):
    return pl.pallas_call(
        merge_kernel,
        in_specs=[VMEM],
        out_specs=VMEM,
        out_shape=jax.ShapeDtypeStruct((16, 16, 128), f32),
        compiler_params=params,
        name="merge",
    )(stats)


def score_block(logits, tokens, log_total, entropy, base, row_start, q):
    lanes = slice(q * 128, q * 128 + 128)
    part = logits[pl.ds(pl.multiple_of(base, 8), PAD), lanes]
    row = lax.broadcasted_iota(jnp.int32, (PAD, 128), 0)
    tok_weight = tokens[0:1, lanes]
    goal = tokens[1:2, lanes].astype(jnp.int32)
    hit = (row + (row_start + base) == goal).astype(f32)
    above = part - log_total[q : q + 1, :]
    probability = jnp.exp(above)
    score = tok_weight * (
        probability - hit + penalty * probability * (above + entropy[q : q + 1, :])
    )
    return jnp.where(row < OWN, score, 0.0).astype(bf16)


def fetch(source, target, sems):
    copies = []
    for block in range(2):
        tokens = slice(block * 512, block * 512 + 512)
        copy = pltpu.make_async_copy(source.at[tokens], target.at[tokens], sems.at[block])
        copy.start()
        copies.append(copy)
    return copies


def away_kernel(place, stats, logits, tokens, hidden, score, totals, fetched, sems):
    copies = fetch(hidden, fetched, sems)
    core = place[0]
    log_total, mean = merged(stats[...])
    entropy = log_total - mean
    totals[:8, :] = log_total
    totals[8:, :] = entropy
    for q in range(PEERS):
        score[:, q * 128 : q * 128 + 128] = score_block(
            logits, tokens, log_total, entropy, (1 - core) * OWN, place[1], q
        )
    for copy in copies:
        copy.wait()


def away_call(place, stats, logits, tokens, hidden):
    return pl.pallas_call(
        away_kernel,
        in_specs=[SMEM, VMEM, VMEM, VMEM, HBM],
        out_specs=[VMEM] * 3,
        out_shape=[
            jax.ShapeDtypeStruct((PAD, TOKENS), bf16),
            jax.ShapeDtypeStruct((16, 128), f32),
            pltpu.VMEM((TOKENS, D), bf16),
        ],
        scratch_shapes=[pltpu.SemaphoreType.DMA((2,))],
        compiler_params=params,
        name="away",
    )(place, stats, logits, tokens, hidden)


def own_kernel(place, totals, logits, tokens, hidden, other, out, fetched, score, sems):
    copies = fetch(other, fetched, sems)
    for q in range(PEERS):
        score[:, q * 128 : q * 128 + 128] = score_block(
            logits, tokens, totals[:8, :], totals[8:, :], place[0] * OWN, place[1], q
        )
    for block in range(4):
        lanes = slice(block * 512, block * 512 + 512)
        out[:, lanes] = jnp.dot(score[...], hidden[:, lanes], preferred_element_type=f32)
    for copy in copies:
        copy.wait()


def own_call(place, totals, logits, tokens, hidden, other):
    return pl.pallas_call(
        own_kernel,
        in_specs=[SMEM] + [VMEM] * 4 + [HBM],
        out_specs=[VMEM] * 2,
        out_shape=[
            jax.ShapeDtypeStruct((PAD, D), f32),
            pltpu.VMEM((TOKENS, D), bf16),
        ],
        scratch_shapes=[
            pltpu.VMEM((PAD, TOKENS), bf16),
            pltpu.SemaphoreType.DMA((2,)),
        ],
        compiler_params=params,
        name="own",
    )(place, totals, logits, tokens, hidden, other)


def split_rows(value):
    high = value.astype(bf16).astype(f32)
    rest = value - high
    middle = rest.astype(bf16).astype(f32)
    return [high, middle, rest - middle]


def join_rows(total, start):
    return total[start : start + 1] + total[start + 1 : start + 2] + total[start + 2 : start + 3]


def grad_kernel(
    place, partial, score, hidden, state, totals, tokens, scaled, sums, grad, table
):
    core = place[0]
    places = [2 * i + core for i in range(8)] + [2 * i + 1 - core for i in range(8)]
    squares = jnp.zeros((PAD, 128), f32)
    for source in range(4):
        block = (source + 2) % 4
        lanes = slice(block * 512, block * 512 + 512)
        start = source * 512
        value = partial[:, lanes] + jnp.dot(
            score[...], hidden[:, start : start + 512], preferred_element_type=f32
        )
        grad[:, lanes] = value
        for i in range(4):
            part = value[:, 128 * i : 128 * i + 128]
            part = part * part
            squares = squares + part
            table[pl.ds(places[4 * block + i], 1), :] = jnp.sum(part, axis=0, keepdims=True)
    diagonal = lax.broadcasted_iota(jnp.int32, (PAD, PAD), 0) == lax.broadcasted_iota(
        jnp.int32, (PAD, PAD), 1
    )
    old = jnp.sum(jnp.where(diagonal, state[...], 0.0), axis=1, keepdims=True)
    row_new = decay_rate * old + (1.0 - decay_rate) * (
        jnp.sum(squares, axis=1, keepdims=True) / D
    )
    scale = jnp.broadcast_to(lax.rsqrt(row_new), (PAD, 128))
    row = lax.broadcasted_iota(jnp.int32, (PAD, 128), 0)
    lane = lax.broadcasted_iota(jnp.int32, (PAD, 128), 1)
    kept = jnp.where((row < OWN) & (lane == 0), jnp.broadcast_to(row_new, (PAD, 128)), 0.0)
    row_total = jnp.sum(kept, axis=0, keepdims=True)
    loss = jnp.zeros((1, 128), f32)
    for q in range(PEERS):
        lanes = slice(128 * q, 128 * q + 128)
        loss = loss + (
            tokens[0:1, lanes]
            * (totals[q : q + 1, :] - penalty * totals[8 + q : 9 + q, :])
            * (1.0 / 256.0)
            - tokens[2:3, lanes]
        )
    table[32:SUMS, :] = jnp.zeros((SUMS - 32, 128), f32)
    for i, line in enumerate(split_rows(row_total) + split_rows(loss)):
        table[32 + i : 33 + i, :] = line
    for i, j in enumerate(places):
        part = grad[:, 128 * i : 128 * i + 128] * scale
        scaled[:, pl.ds(pl.multiple_of(j * 128, 128), 128)] = part
        table[pl.ds(16 + j, 1), :] = jnp.sum(part * part, axis=0, keepdims=True)
    sums[...] = jnp.broadcast_to(table[...].astype(bf16)[None], (32, SUMS, 128))


def grad_call(place, partial, score, hidden, state, totals, tokens):
    return pl.pallas_call(
        grad_kernel,
        in_specs=[SMEM] + [VMEM] * 6,
        out_specs=[VMEM] * 2,
        out_shape=[
            jax.ShapeDtypeStruct((PAD, D), f32),
            jax.ShapeDtypeStruct((32, SUMS, 128), bf16),
        ],
        scratch_shapes=[
            pltpu.VMEM((PAD, D), f32),
            pltpu.VMEM((SUMS, 128), f32),
        ],
        compiler_params=params,
        name="grad",
    )(place, partial, score, hidden, state, totals, tokens)


def add_kernel(sums, out):
    total = jnp.sum(sums[...].astype(f32), axis=0)
    lines = split_rows(join_rows(total, 32)) + split_rows(join_rows(total, 35))
    row = lax.broadcasted_iota(jnp.int32, (SUMS, 128), 0)
    for i, line in enumerate(lines):
        total = jnp.where(row == 32 + i, line, total)
    out[...] = jnp.broadcast_to(total.astype(bf16)[None], (16, SUMS, 128))


def add_call(sums):
    return pl.pallas_call(
        add_kernel,
        in_specs=[VMEM],
        out_specs=VMEM,
        out_shape=jax.ShapeDtypeStruct((16, SUMS, 128), bf16),
        compiler_params=params,
        name="add",
    )(sums)


def update_kernel(sums, state, scaled, out, loss):
    total = jnp.sum(sums[...].astype(f32), axis=0)
    column_new = decay_rate * state[...] + (1.0 - decay_rate) * (total[:16] / V)
    column_scale = lax.rsqrt(column_new)
    row_mean = jnp.broadcast_to(jnp.sum(join_rows(total, 32), keepdims=True) / V, (16, 128))
    square_total = jnp.sum(total[16:32] * column_scale * column_scale, keepdims=True)
    square_total = row_mean * jnp.broadcast_to(square_total, (16, 128))
    update_rms = jnp.sqrt(square_total / (V * D))
    factor = jnp.sqrt(row_mean) * column_scale / jnp.maximum(1.0, update_rms / clip_limit)
    for j in range(16):
        out[j] = (scaled[:OWN, 128 * j : 128 * j + 128] * factor[j : j + 1, :]).astype(bf16)
    loss[...] = jnp.sum(join_rows(total, 35), keepdims=True)


def update_call(sums, state, scaled):
    return pl.pallas_call(
        update_kernel,
        in_specs=[VMEM] * 3,
        out_specs=[VMEM] * 2,
        out_shape=[
            jax.ShapeDtypeStruct((16, OWN, 128), bf16),
            jax.ShapeDtypeStruct((1, 1), f32),
        ],
        compiler_params=params,
        name="update",
    )(sums, state, scaled)


def per_device(hidden, head_weight, targets, segments, loss_mask, row_state, column_state):
    core = lax.axis_index("core")
    chip = lax.axis_index(CHIPS)
    odd = lax.axis_index("z") % 2
    chip_start = chip * CHIP_ROWS
    place = jnp.stack([core, lax.axis_index(MP) * VOC + chip_start, odd]).astype(jnp.int32)
    own_state = lax.dynamic_slice_in_dim(row_state, chip_start + core * OWN, OWN, axis=0)
    own_state = jnp.concatenate([own_state, jnp.ones((PAD - OWN,), f32)]).reshape(1, PAD)
    place, own_state, targets = lax.optimization_barrier((place, own_state, targets))

    groups = [[4 * y + 2 * xh + (xh ^ k) for y in range(4) for xh in range(2)] for k in range(2)]
    first = lax.all_to_all(spread(hidden), PLANE, 0, 0, axis_index_groups=groups)
    last = pack(hidden, head_weight, targets, segments, loss_mask, column_state)
    last, first = lax.optimization_barrier((last, first))
    last = trade(last, CHIPS)
    near = lax.ppermute(first[:5], "z", [(i, i ^ 1) for i in range(16)])
    far = lax.ppermute(first[5:], "z", [(i, (i + 1 if i % 2 else i - 1) % 16) for i in range(16)])
    last_other = swap_cores(last)
    hidden_own, hidden_sent, partial, own_facts = half_call(place, first, near, far, last)
    logits, stats, other_facts = logits_call(hidden_own, partial, last_other)
    stats, hidden_sent = lax.optimization_barrier((stats, hidden_sent))
    tokens, state = tokens_call(place, own_facts, other_facts, logits)
    hidden_other = swap_cores(hidden_sent)
    stats = merge_call(trade(stats, PLANE))
    stats = trade(stats, "z")
    score_away, totals, hidden_own = away_call(place, stats, logits, tokens, hidden_sent)
    score_other = swap_cores(score_away)
    partial, hidden_other = own_call(
        place, totals, logits, tokens, hidden_own, hidden_other
    )
    scaled, sums = grad_call(
        place, partial, score_other, hidden_other, own_state, totals, tokens
    )
    sums = add_call(trade(sums, ("y", "xh", "core", "xl")))
    update, loss = update_call(trade(sums, "z"), state, scaled)
    update_step = trade(update, DP).reshape(VOC, COLS)
    return (update_step, loss.reshape(()))


def solution(mesh):
    fine = Mesh(mesh.devices.reshape(4, 2, 2, 16, 2), AXES)
    return jax.shard_map(
        per_device,
        mesh=fine,
        in_specs=(P(DP, None), P(MP, DP), P(DP), P(DP), P(DP), P(MP), P(DP)),
        out_specs=(P(MP, DP), P()),
        check_vma=False,
    )
```
